512 devices in a mesh: frame: 64 (over z, y), head: 8 (over x, core).
Axes of the slice: x: 4, y: 8, z: 8, core: 2. Of those that a mesh axis runs over, the one named last changes fastest.
Arguments:
- query_space: bfloat16 [64, 512, 3072], P('frame', None, 'head'), may hold values from -48 to 48
- key_space: bfloat16 [64, 512, 3072], P('frame', None, 'head'), may hold values from -12.5 to 12.5
- value_space: bfloat16 [64, 512, 3072], P('frame', None, 'head'), may hold values from -210 to 210
- query_time: bfloat16 [64, 512, 3072], P('frame', None, 'head'), may hold values from -48 to 48
- key_time: bfloat16 [64, 512, 3072], P('frame', None, 'head'), may hold values from -12.5 to 12.5
- cotangent: bfloat16 [64, 512, 3072], P('frame', None, 'head'), may hold values from -6 to 6
- slot_clip: int32 [64], replicated, may hold values from 0 to 5, as said below
- clip_res: int32 [6], replicated, may hold values from 128 to 512, as said below
Outputs:
- mixed: bfloat16 [64, 512, 3072], P('frame', None, 'head')
- grad_query_space: bfloat16 [64, 512, 3072], P('frame', None, 'head')
- grad_key_space: bfloat16 [64, 512, 3072], P('frame', None, 'head')
- grad_value_space: bfloat16 [64, 512, 3072], P('frame', None, 'head')
- grad_query_time: bfloat16 [64, 512, 3072], P('frame', None, 'head')
- grad_key_time: bfloat16 [64, 512, 3072], P('frame', None, 'head')
The draws below stay inside these ranges and needn't reach their ends.
Inputs may be any that keep to these rules, and one draw needn't show every extreme that they name: `slot_clip`: every clip fills two or more frame slots. `clip_res`: A multiple of 128; some clip has each bound.
All inputs are finite; a program needn't handle non-finite values.
Results may differ from the reference program's by a relative error of at most 0.012.
Values may be sent and summed in bfloat16 or wider, within the bound.
No kernel may reach another device: no remote copies, remote signals or barrier semaphores. Data moves between devices by JAX's collectives and lax.ppermute only.
A program may use at most 64 MiB of HBM per device.

```python
import jax
import jax.numpy as jnp
from jax import lax

HEADS = 24
HD = 128
POS = 512
CLIPS = 6
FRAMES = 64


def draw_query_space(key, part):
    key = jax.random.fold_in(key, 21)
    key_main = jax.random.fold_in(key, 0)
    field_shape = (FRAMES, POS, HEADS * HD)
    field = jnp.clip(jax.random.normal(key_main, field_shape, jnp.float32), -4.0, 4.0)
    return field.astype(jnp.bfloat16)


def draw_key_space(key, part):
    key = jax.random.fold_in(key, 22)
    field_shape = (FRAMES, POS, HEADS * HD)
    field = jnp.clip(jax.random.normal(key, field_shape, jnp.float32), -4.0, 4.0)
    return field.astype(jnp.bfloat16)


def draw_query_time(key, part):
    key = jax.random.fold_in(key, 23)
    key_main = jax.random.fold_in(key, 0)
    field_shape = (FRAMES, POS, HEADS * HD)
    field = jnp.clip(jax.random.normal(key_main, field_shape, jnp.float32), -4.0, 4.0)
    return field.astype(jnp.bfloat16)


def draw_key_time(key, part):
    key = jax.random.fold_in(key, 24)
    key_main = jax.random.fold_in(key, 0)
    field_shape = (FRAMES, POS, HEADS * HD)
    field = jnp.clip(jax.random.normal(key_main, field_shape, jnp.float32), -4.0, 4.0)
    return field.astype(jnp.bfloat16)


def draw_value_space(key, part):
    key = jax.random.fold_in(key, 31)
    key_main, key_column, key_row = jax.random.split(key, 3)
    channels = HEADS * HD
    head_place = (jnp.arange(channels) // HD).astype(jnp.float32) / max(HEADS - 1, 1)
    field_shape = (FRAMES, POS, channels)
    row_scale = 10.0 ** (0.5 * jax.random.uniform(key_row, (FRAMES, POS, 1), jnp.float32))
    column_scale = 10.0 ** (0.5 * head_place + 0.5 * jax.random.uniform(key_column, (channels,), jnp.float32))
    field = jnp.clip(jax.random.normal(key_main, field_shape, jnp.float32), -4.0, 4.0)
    return (field * column_scale * row_scale).astype(jnp.bfloat16)


def draw_slot_clip(key, part):
    key = jax.random.fold_in(key, 41)
    key_place, key_left, key_right = jax.random.split(key, 3)
    placing = jax.random.permutation(key_place, FRAMES)
    index_all = jnp.arange(FRAMES, dtype=jnp.int32)
    spare = jnp.minimum(jax.random.randint(key_left, (FRAMES,), 0, CLIPS), jax.random.randint(key_right, (FRAMES,), 0, CLIPS))
    labels = jnp.where(index_all < 2 * CLIPS, index_all // 2, spare).astype(jnp.int32)
    return jnp.zeros((FRAMES,), jnp.int32).at[placing].set(labels)


def draw_clip_res(key, part):
    key = jax.random.fold_in(key, 42)
    key_level, key_full, key_small = jax.random.split(key, 3)
    levels = jax.random.randint(key_level, (CLIPS,), 1, 5)
    widest = jax.random.randint(key_full, (), 0, CLIPS)
    narrowest = (widest + 1 + jax.random.randint(key_small, (), 0, CLIPS - 1)) % CLIPS
    clip_index = jnp.arange(CLIPS)
    levels = jnp.where(clip_index == widest, 4, jnp.where(clip_index == narrowest, 1, levels))
    return (levels * (POS // 4)).astype(jnp.int32)


def shard_levels(rng, dims, cuts, least, largest):
    gain, own = 1.0, jax.random.fold_in(rng, 6)
    for dim, blocks in cuts:
        steps = jnp.exp(jax.random.uniform(jax.random.fold_in(own, dim), (blocks,), jnp.float32, least / len(cuts), largest / len(cuts)))
        gain = gain * jnp.repeat(steps, dims[dim] // blocks).reshape([-1 if axis == dim else 1 for axis in range(len(dims))])
    return gain


def gaussian(stream_key, dims, scale, bound, cuts=(), held_as=jnp.bfloat16):
    entries = jax.random.normal(stream_key, dims, jnp.float32) * scale
    if len(cuts) > 0:
        entries = shard_levels(stream_key, dims, cuts, -0.22, 0.18) * entries
    return jnp.clip(entries, min=-bound, max=bound).astype(held_as)


def setup_inputs(seed: int = 0) -> dict:
    keys = jax.random.split(jax.random.key(seed), 9)
    query_space = draw_query_space(jax.random.fold_in(keys[8], 71), 0)
    key_space = draw_key_space(jax.random.fold_in(keys[8], 71), 0)
    value_space = draw_value_space(jax.random.fold_in(keys[8], 71), 0)
    query_time = draw_query_time(jax.random.fold_in(keys[8], 71), 0)
    key_time = draw_key_time(jax.random.fold_in(keys[8], 71), 0)
    cotangent = gaussian(keys[5], (FRAMES, POS, HEADS * HD), 1.0, 6.0, ((0, 64), (2, 8)))
    slot_clip = draw_slot_clip(jax.random.fold_in(keys[8], 71), 0)
    clip_res = draw_clip_res(jax.random.fold_in(keys[8], 71), 0)
    return {"query_space": query_space, "key_space": key_space, "value_space": value_space, "query_time": query_time, "key_time": key_time, "cotangent": cotangent, "slot_clip": slot_clip, "clip_res": clip_res}


NEGATIVE = -1e+30
EPSILON = 1e-06

def attend_forward(query_rows, key_rows, value_rows, allowed, live_rows, query_label, key_label):
    score_scale = HD ** (-0.5)
    scores = jnp.einsum(query_label + ',' + key_label + '->bhqk', query_rows.astype(jnp.float32), key_rows.astype(jnp.float32)) * score_scale
    scores = jnp.where(allowed, scores, NEGATIVE)
    highest = lax.optimization_barrier(jnp.max(scores, axis=-1, keepdims=True))
    expanded = jnp.exp(scores - highest)
    weights = expanded / lax.optimization_barrier(jnp.sum(expanded, axis=-1, keepdims=True))
    rounded = weights.astype(jnp.bfloat16)
    output = jnp.einsum('bhqk,' + key_label + '->' + query_label, rounded.astype(jnp.float32), value_rows.astype(jnp.float32))
    return (output * live_rows, weights)

def attend_backward(query_rows, key_rows, value_rows, weights, grad_rows, query_label, key_label):
    score_scale = HD ** (-0.5)
    rounded = weights.astype(jnp.bfloat16).astype(jnp.float32)
    grad_value = jnp.einsum('bhqk,' + query_label + '->' + key_label, rounded, grad_rows.astype(jnp.float32))
    grad_weights = jnp.einsum(query_label + ',' + key_label + '->bhqk', grad_rows.astype(jnp.float32), value_rows.astype(jnp.float32))
    inner_sum = lax.optimization_barrier(jnp.sum(weights * grad_weights, axis=-1, keepdims=True))
    grad_scores = (weights * (grad_weights - inner_sum) * score_scale).astype(jnp.bfloat16).astype(jnp.float32)
    grad_query = jnp.einsum('bhqk,' + key_label + '->' + query_label, grad_scores, key_rows.astype(jnp.float32))
    grad_key = jnp.einsum('bhqk,' + query_label + '->' + key_label, grad_scores, query_rows.astype(jnp.float32))
    return (grad_query, grad_key, grad_value)

def split_heads(array):
    return array.reshape(array.shape[:-1] + (HEADS, HD))

def reference(query_space, key_space, value_space, query_time, key_time, cotangent, slot_clip, clip_res):
    frame_count = query_space.shape[0]
    channels = HEADS * HD
    slot_res = clip_res[slot_clip]
    live = jnp.arange(POS, dtype=jnp.int32)[None, :] < slot_res[:, None]

    def space_forward(items):
        query_rows, key_rows, value_rows, live_rows = items
        allowed = live_rows[None, None, None, :]
        live_float = live_rows[None, :, None, None].astype(jnp.float32)
        output, weights = attend_forward(split_heads(query_rows)[None], split_heads(key_rows)[None], split_heads(value_rows)[None], allowed, live_float, 'bqhd', 'bkhd')
        return output[0].reshape(POS, channels)
    space_out = lax.map(space_forward, (query_space, key_space, value_space, live))
    inverse_rms = lax.rsqrt(lax.optimization_barrier(jnp.sum(space_out * space_out, axis=-1)) / channels + EPSILON)
    normed_full = space_out * inverse_rms[..., None]
    normed = normed_full.astype(jnp.bfloat16)
    grad_in = jnp.where(live[..., None], cotangent, jnp.zeros_like(cotangent))
    blocks = POS // 8
    same_clip = slot_clip[:, None] == slot_clip[None, :]
    diagonal = jnp.eye(frame_count, dtype=bool)

    def to_blocks(array):
        return array.reshape(frame_count, blocks, 8, channels).transpose(1, 0, 2, 3)
    live_blocks = live.reshape(frame_count, blocks, 8).transpose(1, 0, 2)

    def time_pass(items):
        query_rows, key_rows, value_rows, grad_rows, live_rows = items
        allowed = same_clip[None, None] & (live_rows.T[:, None, None, :] | diagonal[None, None])
        live_float = live_rows[:, :, None, None].astype(jnp.float32)
        output, weights = attend_forward(split_heads(query_rows), split_heads(key_rows), split_heads(value_rows), allowed, live_float, 'qbhd', 'kbhd')
        grad_query, grad_key, grad_value = attend_backward(split_heads(query_rows), split_heads(key_rows), split_heads(value_rows), weights, split_heads(grad_rows), 'qbhd', 'kbhd')
        shape_rows = (frame_count, 8, channels)
        return (output.reshape(shape_rows), grad_query.reshape(shape_rows), grad_key.reshape(shape_rows), grad_value.reshape(shape_rows))
    time_results = lax.map(time_pass, (to_blocks(query_time), to_blocks(key_time), to_blocks(normed), to_blocks(grad_in), live_blocks))

    def from_blocks(array):
        return array.transpose(1, 0, 2, 3).reshape(frame_count, POS, channels).astype(jnp.bfloat16)
    time_out = from_blocks(time_results[0])
    grad_query_time = from_blocks(time_results[1])
    grad_key_time = from_blocks(time_results[2])
    grad_value_time = from_blocks(time_results[3])
    mixed = (normed.astype(jnp.float32) + time_out.astype(jnp.float32)).astype(jnp.bfloat16)
    grad_norm = grad_in.astype(jnp.float32) + grad_value_time.astype(jnp.float32)
    inner_norm = lax.optimization_barrier(jnp.sum(grad_norm * normed_full, axis=-1))
    grad_space_out = (inverse_rms[..., None] * (grad_norm - normed_full * (inner_norm / channels)[..., None])).astype(jnp.bfloat16)

    def space_backward(items):
        query_rows, key_rows, value_rows, live_rows, grad_rows = items
        allowed = live_rows[None, None, None, :]
        live_float = live_rows[None, :, None, None].astype(jnp.float32)
        query_heads = split_heads(query_rows)[None]
        key_heads = split_heads(key_rows)[None]
        value_heads = split_heads(value_rows)[None]
        output, weights = attend_forward(query_heads, key_heads, value_heads, allowed, live_float, 'bqhd', 'bkhd')
        grad_query, grad_key, grad_value = attend_backward(query_heads, key_heads, value_heads, weights, split_heads(grad_rows)[None], 'bqhd', 'bkhd')
        return (grad_query[0].reshape(POS, channels).astype(jnp.bfloat16), grad_key[0].reshape(POS, channels).astype(jnp.bfloat16), grad_value[0].reshape(POS, channels).astype(jnp.bfloat16))
    grad_query_space, grad_key_space, grad_value_space = lax.map(space_backward, (query_space, key_space, value_space, live, grad_space_out))
    return (mixed, grad_query_space, grad_key_space, grad_value_space, grad_query_time, grad_key_time)
```

```python
import jax
import jax.numpy as jnp
from jax import lax
from jax.experimental import pallas as pl
from jax.experimental.pallas import tpu as pltpu
from jax.sharding import PartitionSpec as P

HD = 128
NEGATIVE = -1e30
EPSILON = 1e-06
LOG2E = 1.4426950408889634
F32 = jnp.float32
BF16 = jnp.bfloat16
VMEM_BYTES = 32 * 1024 * 1024


def dot(a, b, ca, cb):
    return lax.dot_general(a, b, (((ca,), (cb,)), ((), ())), preferred_element_type=F32)


def softmax_keys_first(q, k, q_mask, k_mask):
    scale = HD ** (-0.5)
    scores = dot(
        jnp.concatenate([k, k_mask], axis=1), jnp.concatenate([q, q_mask], axis=1), 1, 1
    )
    highest = jnp.max(scores, axis=0, keepdims=True)
    expanded = jnp.exp2((scores - highest) * (scale * LOG2E))
    return expanded, 1.0 / jnp.sum(expanded, axis=0, keepdims=True)


def softmax_queries_first(q, k, q_mask, k_mask):
    scale = HD ** (-0.5)
    scores = dot(
        jnp.concatenate([q, q_mask], axis=1), jnp.concatenate([k, k_mask], axis=1), 1, 1
    )
    highest = jnp.max(scores, axis=1, keepdims=True)
    expanded = jnp.exp2((scores - highest) * (scale * LOG2E))
    return expanded, 1.0 / jnp.sum(expanded, axis=1, keepdims=True)


def pack_kernel(a_ref, b_ref, c_ref, out_ref):
    out_ref[:, :HD] = a_ref[...]
    out_ref[:, HD : 2 * HD] = b_ref[...]
    out_ref[:, 2 * HD :] = c_ref[...]


def space_forward_kernel(q_ref, k_ref, v_ref, q_mask_ref, k_mask_ref, live_ref, out_ref):
    expanded, inverse = softmax_queries_first(
        q_ref[...], k_ref[...], q_mask_ref[...], k_mask_ref[...]
    )
    weights = (expanded * inverse).astype(BF16)
    out_ref[...] = dot(weights, v_ref[...], 1, 0) * live_ref[...]


def space_backward_kernel(
    q_ref, k_ref, v_ref, g_ref, q_mask_ref, k_mask_ref, gq_ref, gk_ref, gv_ref
):
    scale = HD ** (-0.5)
    q, k, v, g = q_ref[...], k_ref[...], v_ref[...], g_ref[...]
    expanded, inverse = softmax_keys_first(q, k, q_mask_ref[...], k_mask_ref[...])
    weights = expanded * inverse
    gv_ref[...] = dot(weights.astype(BF16), g, 1, 0).astype(BF16)
    grad_weights = dot(v, g, 1, 1)
    inner = jnp.sum(weights * grad_weights, axis=0, keepdims=True)
    grad_scores = (weights * (grad_weights - inner) * scale).astype(BF16)
    gk_ref[...] = dot(grad_scores, q, 1, 0).astype(BF16)
    gq_ref[...] = dot(grad_scores, k, 0, 0).astype(BF16)


def time_value_kernel(moved_ref, normed_ref, q_mask_ref, k_mask_ref, live_ref, out_ref):
    q, k, g = moved_ref[:, :HD], moved_ref[:, HD : 2 * HD], moved_ref[:, 2 * HD :]
    expanded, inverse = softmax_keys_first(q, k, q_mask_ref[...], k_mask_ref[...])
    weights = (expanded * (inverse * live_ref[...])).astype(BF16)
    out_ref[:, :HD] = normed_ref[...]
    out_ref[:, HD:] = dot(weights, g, 1, 0).astype(BF16)


def time_weights_kernel(moved_ref, q_mask_ref, k_mask_ref, live_ref, weights_ref):
    q, k = moved_ref[:, :HD], moved_ref[:, HD : 2 * HD]
    expanded, inverse = softmax_keys_first(q, k, q_mask_ref[...], k_mask_ref[...])
    weights_ref[0] = expanded * (inverse * live_ref[...])


def time_rest_kernel(moved_ref, normed_ref, weights_ref, out_ref):
    scale = HD ** (-0.5)
    q, k, g = moved_ref[:, :HD], moved_ref[:, HD : 2 * HD], moved_ref[:, 2 * HD :]
    v = normed_ref[...]
    weights = weights_ref[0]
    out_ref[:, :HD] = dot(weights.astype(BF16), v, 0, 0).astype(BF16)
    grad_weights = dot(v, g, 1, 1)
    inner = jnp.sum(weights * grad_weights, axis=0, keepdims=True)
    grad_scores = (weights * (grad_weights - inner) * scale).astype(BF16)
    out_ref[:, HD : 2 * HD] = dot(grad_scores, k, 0, 0).astype(BF16)
    out_ref[:, 2 * HD :] = dot(grad_scores, q, 1, 0).astype(BF16)


def finish_kernel(back_ref, normed_ref, mixed_ref, gq_ref, gk_ref):
    mixed_ref[...] = (
        normed_ref[...].astype(F32) + back_ref[:, :HD].astype(F32)
    ).astype(BF16)
    gq_ref[...] = back_ref[:, HD : 2 * HD]
    gk_ref[...] = back_ref[:, 2 * HD :]


def per_device(
    query_space, key_space, value_space, query_time, key_time, cotangent, slot_clip, clip_res
):
    _, rows, channels = query_space.shape
    head_count = channels // HD
    frames = slot_clip.shape[0]
    full_channels = channels * lax.axis_size("head")
    positions_here = rows // lax.axis_size("frame")
    here = lax.axis_index("frame")

    def head_block(width=1):
        return pl.BlockSpec((rows, width * HD), lambda h: (0, h))

    def shared(shape):
        return pl.BlockSpec(shape, lambda h: (0,) * len(shape))

    def call(kernel, in_specs, out_specs, out_shape, flops=0, traffic=0):
        return pl.pallas_call(
            kernel,
            grid=(head_count,),
            in_specs=in_specs,
            out_specs=out_specs,
            out_shape=out_shape,
            compiler_params=pltpu.CompilerParams(
                dimension_semantics=("arbitrary",), vmem_limit_bytes=VMEM_BYTES
            ),
            cost_estimate=pl.CostEstimate(
                flops=flops, bytes_accessed=traffic, transcendentals=0
            ),
        )

    def exchange(array):
        width = array.shape[-1]
        blocks = array.reshape(frames, positions_here, width)
        moved = lax.all_to_all(blocks, "frame", split_axis=0, concat_axis=0, tiled=True)
        return moved.reshape(rows, width)

    whole = jax.ShapeDtypeStruct((rows, channels), BF16)
    product = 2 * rows * rows * HD * head_count
    size = rows * channels * 2

    q_space, k_space, v_space = query_space[0], key_space[0], value_space[0]

    packed = call(
        pack_kernel,
        [head_block()] * 3,
        head_block(3),
        jax.ShapeDtypeStruct((rows, 3 * channels), BF16),
        traffic=6 * size,
    )(query_time[0], key_time[0], cotangent[0])
    moved = exchange(packed)

    clip_match = slot_clip[:, None] == jnp.arange(clip_res.shape[0], dtype=jnp.int32)[None, :]
    slot_res = jnp.sum(jnp.where(clip_match, clip_res[None, :], 0), axis=1)
    local_res = lax.dynamic_slice_in_dim(slot_res, here, 1, 0)
    live_space = jnp.arange(rows, dtype=jnp.int32) < local_res
    column = jnp.arange(HD, dtype=jnp.int32)[None, :]
    space_q_mask = jnp.broadcast_to(column == 0, (rows, HD)).astype(BF16)
    space_k_mask = jnp.where(live_space[:, None], 0.0, NEGATIVE).astype(BF16)
    space_k_mask = jnp.broadcast_to(space_k_mask, (rows, HD))
    place = jnp.arange(positions_here, dtype=jnp.int32)[None, :]
    live_time = (here * positions_here + place) < slot_res[:, None]
    group = slot_clip[:, None] * positions_here + place
    group = group.reshape(rows, 1)
    time_q_mask = (column == group).astype(BF16)
    time_k_mask = jnp.where((column == group) & live_time.reshape(rows, 1), 0.0, NEGATIVE)
    time_k_mask = time_k_mask.astype(BF16)
    live_row = live_time.reshape(1, rows).astype(F32)

    mask_spec = shared((rows, HD))
    space_out = call(
        space_forward_kernel,
        [head_block()] * 3 + [mask_spec, mask_spec, shared((rows, 1))],
        head_block(),
        jax.ShapeDtypeStruct((rows, channels), F32),
        flops=3 * product,
        traffic=5 * size,
    )(q_space, k_space, v_space, space_q_mask, space_k_mask, live_space[:, None].astype(F32))
    square_sum = lax.psum(jnp.sum(space_out * space_out, axis=-1), "head")
    inverse_rms = lax.rsqrt(square_sum / full_channels + EPSILON)
    normed_full = space_out * inverse_rms[:, None]
    normed = normed_full.astype(BF16)

    pair = call(
        time_value_kernel,
        [head_block(3), head_block(), mask_spec, mask_spec, shared((1, rows))],
        head_block(2),
        jax.ShapeDtypeStruct((rows, 2 * channels), BF16),
        flops=3 * product,
        traffic=6 * size,
    )(moved, normed, time_q_mask, time_k_mask, live_row)
    pair_moved = exchange(pair)
    weights_spec = pl.BlockSpec((1, rows, rows), lambda h: (h, 0, 0))
    time_weights = call(
        time_weights_kernel,
        [head_block(3), mask_spec, mask_spec, shared((1, rows))],
        weights_spec,
        jax.ShapeDtypeStruct((head_count, rows, rows), F32),
        flops=2 * product,
        traffic=8 * size,
    )(moved, time_q_mask, time_k_mask, live_row)
    results = call(
        time_rest_kernel,
        [head_block(3), pl.BlockSpec((rows, HD), lambda h: (0, 2 * h)), weights_spec],
        head_block(3),
        jax.ShapeDtypeStruct((rows, 3 * channels), BF16),
        flops=4 * product,
        traffic=12 * size,
    )(moved, pair_moved, time_weights)
    back = exchange(results)

    grad_value_back = pair_moved.reshape(rows, head_count, 2, HD)[:, :, 1].reshape(rows, channels)
    grad_in = jnp.where(live_space[:, None], cotangent[0], jnp.zeros_like(cotangent[0]))
    grad_norm = grad_in.astype(F32) + grad_value_back.astype(F32)
    inner_norm = lax.psum(jnp.sum(grad_norm * normed_full, axis=-1), "head")
    grad_space_out = (
        inverse_rms[:, None] * (grad_norm - normed_full * (inner_norm / full_channels)[:, None])
    ).astype(BF16)
    grad_query_space, grad_key_space, grad_value_space = call(
        space_backward_kernel,
        [head_block()] * 4 + [mask_spec, mask_spec],
        [head_block()] * 3,
        [whole] * 3,
        flops=6 * product,
        traffic=7 * size,
    )(q_space, k_space, v_space, grad_space_out, space_q_mask, space_k_mask)

    mixed, grad_query_time, grad_key_time = call(
        finish_kernel,
        [head_block(3), head_block()],
        [head_block()] * 3,
        [whole] * 3,
        traffic=7 * size,
    )(back, normed)
    return (
        mixed[None],
        grad_query_space[None],
        grad_key_space[None],
        grad_value_space[None],
        grad_query_time[None],
        grad_key_time[None],
    )


def solution(mesh):
    sharded = P("frame", None, "head")
    return jax.shard_map(
        per_device,
        mesh=mesh,
        in_specs=(sharded,) * 6 + (P(), P()),
        out_specs=(sharded,) * 6,
        check_vma=False,
    )
```

```python
import jax
import jax.numpy as jnp
from jax import lax
from jax.experimental import pallas as pl
from jax.experimental.pallas import tpu as pltpu
from jax.sharding import PartitionSpec as P

HD = 128
NEGATIVE = -1e30
EPSILON = 1e-06
LOG2E = 1.4426950408889634
F32 = jnp.float32
BF16 = jnp.bfloat16
VMEM_BYTES = 24 * 1024 * 1024
LOWEST = -3e38


def dot(a, b, ca, cb):
    return lax.dot_general(a, b, (((ca,), (cb,)), ((), ())), preferred_element_type=F32)


def softmax_keys_first(q, k, q_mask, k_mask):
    scale = HD ** (-0.5)
    scores = dot(
        jnp.concatenate([k, k_mask], axis=1), jnp.concatenate([q, q_mask], axis=1), 1, 1
    )
    highest = jnp.max(scores, axis=0, keepdims=True)
    expanded = jnp.exp2((scores - highest) * (scale * LOG2E))
    return expanded, 1.0 / jnp.sum(expanded, axis=0, keepdims=True)


def softmax_queries_first(q, k, q_mask, k_mask):
    scale = HD ** (-0.5)
    scores = dot(
        jnp.concatenate([q, q_mask], axis=1), jnp.concatenate([k, k_mask], axis=1), 1, 1
    )
    highest = jnp.max(scores, axis=1, keepdims=True)
    expanded = jnp.exp2((scores - highest) * (scale * LOG2E))
    return expanded, 1.0 / jnp.sum(expanded, axis=1, keepdims=True)


def pack_kernel(a_ref, b_ref, c_ref, out_ref, held, in_sem, out_sem):
    width = a_ref.shape[1]
    loads, stores = [], []
    for i, ref in enumerate((a_ref, b_ref, c_ref)):
        loads.append(pltpu.make_async_copy(ref, held.at[i], in_sem.at[i]))
        stores.append(
            pltpu.make_async_copy(
                held.at[i], out_ref.at[:, pl.ds(i * width, width)], out_sem.at[i]
            )
        )
    for load in loads:
        load.start()
    for load, store in zip(loads, stores):
        load.wait()
        store.start()
    for store in stores:
        store.wait()


def space_forward_kernel(q_ref, k_ref, v_ref, q_mask_ref, k_mask_ref, live_ref, out_ref):
    expanded, inverse = softmax_queries_first(
        q_ref[...], k_ref[...], q_mask_ref[...], k_mask_ref[...]
    )
    weights = (expanded * inverse).astype(BF16)
    out_ref[...] = dot(weights, v_ref[...], 1, 0) * live_ref[...]


def space_backward_kernel(
    q_ref, k_ref, v_ref, g_ref, q_mask_ref, k_mask_ref, gq_ref, gk_ref, gv_ref
):
    scale = HD ** (-0.5)
    q, k, v, g = q_ref[...], k_ref[...], v_ref[...], g_ref[...]
    expanded, inverse = softmax_keys_first(q, k, q_mask_ref[...], k_mask_ref[...])
    weights = expanded * inverse
    gv_ref[...] = dot(weights.astype(BF16), g, 1, 0).astype(BF16)
    grad_weights = dot(v, g, 1, 1)
    inner = jnp.sum(weights * grad_weights, axis=0, keepdims=True)
    grad_scores = (weights * (grad_weights - inner) * scale).astype(BF16)
    gk_ref[...] = dot(grad_scores, q, 1, 0).astype(BF16)
    gq_ref[...] = dot(grad_scores, k, 0, 0).astype(BF16)


def time_value_kernel(
    moved_ref, normed_ref, q_mask_ref, k_mask_ref, live_ref, out_ref, shift_ref, held, sem
):
    scale = HD ** (-0.5) * LOG2E
    width = normed_ref.shape[1]
    heads = width // HD
    copies = [pltpu.make_async_copy(normed_ref, out_ref.at[:, pl.ds(0, width)], sem.at[heads])]
    copies[0].start()
    q_mask, k_mask, live = q_mask_ref[...], k_mask_ref[...], live_ref[...]
    for h in range(heads):
        q, k, g = (
            moved_ref[:, j * width + h * HD : j * width + (h + 1) * HD] for j in range(3)
        )
        scores = dot(
            jnp.concatenate([k, k_mask], axis=1), jnp.concatenate([q, q_mask], axis=1), 1, 1
        )
        highest = jnp.max(scores, axis=0, keepdims=True)
        expanded = jnp.exp2((scores - highest) * scale)
        inverse = 1.0 / jnp.sum(expanded, axis=0, keepdims=True)
        weights = (expanded * (inverse * live)).astype(BF16)
        shift_ref[h : h + 1, :] = jnp.where(
            live > 0, jnp.log2(inverse) - highest * scale, LOWEST
        )
        held[h] = dot(weights, g, 1, 0).astype(BF16)
        copies.append(
            pltpu.make_async_copy(
                held.at[h], out_ref.at[:, pl.ds(width + h * HD, HD)], sem.at[h]
            )
        )
        copies[-1].start()
    for copy in copies:
        copy.wait()


def time_rest_kernel(
    moved_ref, pair_ref, q_mask_ref, k_mask_ref, shift_ref, out_ref, held, sem
):
    scale = HD ** (-0.5)
    width = pair_ref.shape[1] // 2
    heads = width // HD
    copies = []
    q_mask, k_mask = q_mask_ref[...], k_mask_ref[...]
    for h in range(heads):
        q, k, g = (
            moved_ref[:, j * width + h * HD : j * width + (h + 1) * HD] for j in range(3)
        )
        v = pair_ref[:, h * HD : (h + 1) * HD]
        scores = dot(
            jnp.concatenate([k, k_mask], axis=1), jnp.concatenate([q, q_mask], axis=1), 1, 1
        )
        weights = jnp.exp2(scores * (scale * LOG2E) + shift_ref[h : h + 1, :])
        time_out = dot(weights.astype(BF16), v, 0, 0)
        grad_weights = dot(v, g, 1, 1)
        inner = jnp.sum(weights * grad_weights, axis=0, keepdims=True)
        grad_scores = (weights * (grad_weights - inner)).astype(BF16)
        grad_query = dot(grad_scores, k, 0, 0) * scale
        grad_key = dot(grad_scores, q, 1, 0) * scale
        for j, result in enumerate((time_out, grad_query, grad_key)):
            held[j, h] = result.astype(BF16)
            copies.append(
                pltpu.make_async_copy(
                    held.at[j, h], out_ref.at[:, pl.ds(j * width + h * HD, HD)], sem.at[j, h]
                )
            )
            copies[-1].start()
    for copy in copies:
        copy.wait()


def finish_kernel(back_ref, normed_ref, mixed_ref, gq_ref, gk_ref, held, sem):
    width = normed_ref.shape[1]
    copies = [
        pltpu.make_async_copy(back_ref.at[:, pl.ds(width, width)], gq_ref, sem.at[0]),
        pltpu.make_async_copy(back_ref.at[:, pl.ds(2 * width, width)], gk_ref, sem.at[1]),
        pltpu.make_async_copy(held, mixed_ref, sem.at[2]),
    ]
    copies[0].start()
    copies[1].start()
    held[...] = (normed_ref[...].astype(F32) + back_ref[:, :width].astype(F32)).astype(BF16)
    copies[2].start()
    for copy in copies:
        copy.wait()


def per_device(
    query_space, key_space, value_space, query_time, key_time, cotangent, slot_clip, clip_res
):
    _, rows, channels = query_space.shape
    head_count = channels // HD
    frames = slot_clip.shape[0]
    full_channels = channels * lax.axis_size("head")
    positions_here = rows // lax.axis_size("frame")
    here = lax.axis_index("frame")
    side = 8

    def head_block(width=1):
        return pl.BlockSpec((rows, width * HD), lambda h: (0, h))

    def shared(shape):
        return pl.BlockSpec(shape, lambda h: (0,) * len(shape))

    def call(kernel, in_specs, out_specs, out_shape, flops=0, traffic=0):
        return pl.pallas_call(
            kernel,
            grid=(head_count,),
            in_specs=in_specs,
            out_specs=out_specs,
            out_shape=out_shape,
            compiler_params=pltpu.CompilerParams(
                dimension_semantics=("arbitrary",), vmem_limit_bytes=VMEM_BYTES
            ),
            cost_estimate=pl.CostEstimate(
                flops=flops, bytes_accessed=traffic, transcendentals=0
            ),
        )

    def local(kernel, in_specs, out_specs, out_shape, scratch, flops=0, traffic=0):
        return pl.pallas_call(
            kernel,
            in_specs=in_specs,
            out_specs=out_specs,
            out_shape=out_shape,
            scratch_shapes=scratch,
            compiler_params=pltpu.CompilerParams(vmem_limit_bytes=VMEM_BYTES),
            cost_estimate=pl.CostEstimate(
                flops=flops, bytes_accessed=traffic, transcendentals=0
            ),
        )

    order = [z * side + y for y in range(side) for z in range(side)]
    block_here = lax.rem(here, side) * side + lax.div(here, side)

    def ordered(per_frame):
        return per_frame.reshape(side, side).T.reshape(frames)

    def exchange(array):
        width = array.shape[-1]
        blocks = array.reshape(frames, positions_here, width)
        moved = lax.all_to_all(
            blocks, "frame", split_axis=0, concat_axis=0, tiled=True, axis_index_groups=[order]
        )
        return moved.reshape(rows, width)

    whole = jax.ShapeDtypeStruct((rows, channels), BF16)
    product = 2 * rows * rows * HD * head_count
    size = rows * channels * 2

    q_space, k_space, v_space = query_space[0], key_space[0], value_space[0]

    hbm, vmem = pl.BlockSpec(memory_space=pltpu.HBM), pl.BlockSpec(memory_space=pltpu.VMEM)
    dma = pltpu.SemaphoreType.DMA
    packed = local(
        pack_kernel,
        [hbm] * 3,
        hbm,
        jax.ShapeDtypeStruct((rows, 3 * channels), BF16),
        [pltpu.VMEM((3, rows, channels), BF16), dma((3,)), dma((3,))],
        traffic=6 * size,
    )(query_time[0], key_time[0], cotangent[0])
    moved = exchange(packed)

    clip_match = slot_clip[:, None] == jnp.arange(clip_res.shape[0], dtype=jnp.int32)[None, :]
    slot_res = jnp.sum(jnp.where(clip_match, clip_res[None, :], 0), axis=1)
    local_res = lax.dynamic_slice_in_dim(slot_res, here, 1, 0)
    live_space = jnp.arange(rows, dtype=jnp.int32) < local_res
    column = jnp.arange(HD, dtype=jnp.int32)[None, :]
    space_q_mask = jnp.broadcast_to(column == 0, (rows, HD)).astype(BF16)
    space_k_mask = jnp.where(live_space[:, None], 0.0, NEGATIVE).astype(BF16)
    space_k_mask = jnp.broadcast_to(space_k_mask, (rows, HD))
    place = jnp.arange(positions_here, dtype=jnp.int32)[None, :]
    live_time = (block_here * positions_here + place) < ordered(slot_res)[:, None]
    group = ordered(slot_clip)[:, None] * positions_here + place
    group = group.reshape(rows, 1)
    time_q_mask = (column == group).astype(BF16)
    time_k_mask = jnp.where((column == group) & live_time.reshape(rows, 1), 0.0, NEGATIVE)
    time_k_mask = time_k_mask.astype(BF16)
    live_row = live_time.reshape(1, rows).astype(F32)

    mask_spec = shared((rows, HD))
    space_out = call(
        space_forward_kernel,
        [head_block()] * 3 + [mask_spec, mask_spec, shared((rows, 1))],
        head_block(),
        jax.ShapeDtypeStruct((rows, channels), F32),
        flops=3 * product,
        traffic=5 * size,
    )(q_space, k_space, v_space, space_q_mask, space_k_mask, live_space[:, None].astype(F32))
    square_sum = lax.psum(jnp.sum(space_out * space_out, axis=-1), "head")
    inverse_rms = lax.rsqrt(square_sum / full_channels + EPSILON)
    normed_full = space_out * inverse_rms[:, None]
    normed = normed_full.astype(BF16)

    pair, shift = local(
        time_value_kernel,
        [vmem] * 5,
        [hbm, vmem],
        [
            jax.ShapeDtypeStruct((rows, 2 * channels), BF16),
            jax.ShapeDtypeStruct((8, rows), F32),
        ],
        [pltpu.VMEM((head_count, rows, HD), BF16), dma((head_count + 1,))],
        flops=3 * product,
        traffic=6 * size,
    )(moved, normed, time_q_mask, time_k_mask, live_row)
    pair_moved = exchange(pair)
    results = local(
        time_rest_kernel,
        [vmem] * 5,
        hbm,
        jax.ShapeDtypeStruct((rows, 3 * channels), BF16),
        [pltpu.VMEM((3, head_count, rows, HD), BF16), dma((3, head_count))],
        flops=6 * product,
        traffic=8 * size,
    )(moved, pair_moved, time_q_mask, time_k_mask, shift)
    back = exchange(results)

    grad_value_back = pair_moved[:, channels:]
    grad_in = jnp.where(live_space[:, None], cotangent[0], jnp.zeros_like(cotangent[0]))
    grad_norm = grad_in.astype(F32) + grad_value_back.astype(F32)
    inner_norm = lax.psum(jnp.sum(grad_norm * normed_full, axis=-1), "head")
    grad_space_out = (
        inverse_rms[:, None] * (grad_norm - normed_full * (inner_norm / full_channels)[:, None])
    ).astype(BF16)
    grad_query_space, grad_key_space, grad_value_space = call(
        space_backward_kernel,
        [head_block()] * 4 + [mask_spec, mask_spec],
        [head_block()] * 3,
        [whole] * 3,
        flops=6 * product,
        traffic=7 * size,
    )(q_space, k_space, v_space, grad_space_out, space_q_mask, space_k_mask)

    mixed, grad_query_time, grad_key_time = local(
        finish_kernel,
        [vmem] * 2,
        [hbm] * 3,
        [whole] * 3,
        [pltpu.VMEM((rows, channels), BF16), dma((3,))],
        traffic=7 * size,
    )(back, normed)
    return (
        mixed[None],
        grad_query_space[None],
        grad_key_space[None],
        grad_value_space[None],
        grad_query_time[None],
        grad_key_time[None],
    )


def solution(mesh):
    sharded = P("frame", None, "head")
    return jax.shard_map(
        per_device,
        mesh=mesh,
        in_specs=(sharded,) * 6 + (P(), P()),
        out_specs=(sharded,) * 6,
        check_vma=False,
    )
```

```python
import jax
import jax.numpy as jnp
from jax import lax
from jax.experimental import pallas as pl
from jax.experimental.pallas import tpu as pltpu
from jax.sharding import PartitionSpec as P

HD = 128
NEGATIVE = -1e30
EPSILON = 1e-06
LOG2E = 1.4426950408889634
F32 = jnp.float32
BF16 = jnp.bfloat16
VMEM_BYTES = 24 * 1024 * 1024
LOWEST = -3e38
Z_PLACES = (6, 2, 0, 4, 7, 3, 1, 5)
Y_PLACES = (4, 5, 6, 7, 0, 1, 2, 3)


def dot(a, b, ca, cb):
    return lax.dot_general(a, b, (((ca,), (cb,)), ((), ())), preferred_element_type=F32)


def softmax_keys_first(q, k, q_mask, k_mask):
    scale = HD ** (-0.5)
    scores = dot(
        jnp.concatenate([k, k_mask], axis=1), jnp.concatenate([q, q_mask], axis=1), 1, 1
    )
    highest = jnp.max(scores, axis=0, keepdims=True)
    expanded = jnp.exp2((scores - highest) * (scale * LOG2E))
    return expanded, 1.0 / jnp.sum(expanded, axis=0, keepdims=True)


def softmax_queries_first(q, k, q_mask, k_mask):
    scale = HD ** (-0.5)
    scores = dot(
        jnp.concatenate([q, q_mask], axis=1), jnp.concatenate([k, k_mask], axis=1), 1, 1
    )
    highest = jnp.max(scores, axis=1, keepdims=True)
    expanded = jnp.exp2((scores - highest) * (scale * LOG2E))
    return expanded, 1.0 / jnp.sum(expanded, axis=1, keepdims=True)


def pack_kernel(a_ref, b_ref, c_ref, out_ref, held, in_sem, out_sem):
    width = a_ref.shape[1]
    loads, stores = [], []
    for i, ref in enumerate((a_ref, b_ref, c_ref)):
        loads.append(pltpu.make_async_copy(ref, held.at[i], in_sem.at[i]))
        stores.append(
            pltpu.make_async_copy(
                held.at[i], out_ref.at[:, pl.ds(i * width, width)], out_sem.at[i]
            )
        )
    for load in loads:
        load.start()
    for load, store in zip(loads, stores):
        load.wait()
        store.start()
    for store in stores:
        store.wait()


def space_forward_kernel(q_ref, k_ref, v_ref, q_mask_ref, k_mask_ref, live_ref, out_ref):
    expanded, inverse = softmax_queries_first(
        q_ref[...], k_ref[...], q_mask_ref[...], k_mask_ref[...]
    )
    weights = (expanded * inverse).astype(BF16)
    out_ref[...] = dot(weights, v_ref[...], 1, 0) * live_ref[...]


def space_backward_kernel(
    q_ref, k_ref, v_ref, g_ref, q_mask_ref, k_mask_ref, gq_ref, gk_ref, gv_ref
):
    scale = HD ** (-0.5)
    q, k, v, g = q_ref[...], k_ref[...], v_ref[...], g_ref[...]
    expanded, inverse = softmax_keys_first(q, k, q_mask_ref[...], k_mask_ref[...])
    weights = expanded * inverse
    gv_ref[...] = dot(weights.astype(BF16), g, 1, 0).astype(BF16)
    grad_weights = dot(v, g, 1, 1)
    inner = jnp.sum(weights * grad_weights, axis=0, keepdims=True)
    grad_scores = (weights * (grad_weights - inner) * scale).astype(BF16)
    gk_ref[...] = dot(grad_scores, q, 1, 0).astype(BF16)
    gq_ref[...] = dot(grad_scores, k, 0, 0).astype(BF16)


def time_value_kernel(
    moved_ref, normed_ref, q_mask_ref, k_mask_ref, live_ref, out_ref, shift_ref
):
    scale = HD ** (-0.5) * LOG2E
    width = normed_ref.shape[1]
    out_ref[:, :width] = normed_ref[...]
    q_mask, k_mask, live = q_mask_ref[...], k_mask_ref[...], live_ref[...]
    for h in range(width // HD):
        q, k, g = (
            moved_ref[:, j * width + h * HD : j * width + (h + 1) * HD] for j in range(3)
        )
        scores = dot(
            jnp.concatenate([k, k_mask], axis=1), jnp.concatenate([q, q_mask], axis=1), 1, 1
        )
        highest = jnp.max(scores, axis=0, keepdims=True)
        expanded = jnp.exp2((scores - highest) * scale)
        inverse = 1.0 / jnp.sum(expanded, axis=0, keepdims=True)
        weights = (expanded * (inverse * live)).astype(BF16)
        shift_ref[h : h + 1, :] = jnp.where(
            live > 0, jnp.log2(inverse) - highest * scale, LOWEST
        )
        out_ref[:, width + h * HD : width + (h + 1) * HD] = dot(weights, g, 1, 0).astype(BF16)


def time_rest_kernel(
    moved_ref, pair_ref, q_mask_ref, k_mask_ref, shift_ref, out_ref, held, sem
):
    scale = HD ** (-0.5)
    width = pair_ref.shape[1] // 2
    heads = width // HD
    copies = []
    q_mask, k_mask = q_mask_ref[...], k_mask_ref[...]
    for h in range(heads):
        q, k, g = (
            moved_ref[:, j * width + h * HD : j * width + (h + 1) * HD] for j in range(3)
        )
        v = pair_ref[:, h * HD : (h + 1) * HD]
        scores = dot(
            jnp.concatenate([k, k_mask], axis=1), jnp.concatenate([q, q_mask], axis=1), 1, 1
        )
        weights = jnp.exp2(scores * (scale * LOG2E) + shift_ref[h : h + 1, :])
        time_out = dot(weights.astype(BF16), v, 0, 0)
        grad_weights = dot(v, g, 1, 1)
        inner = jnp.sum(weights * grad_weights, axis=0, keepdims=True)
        grad_scores = (weights * (grad_weights - inner)).astype(BF16)
        grad_query = dot(grad_scores, k, 0, 0) * scale
        grad_key = dot(grad_scores, q, 1, 0) * scale
        for j, result in enumerate((time_out, grad_query, grad_key)):
            held[j, h] = result.astype(BF16)
            copies.append(
                pltpu.make_async_copy(
                    held.at[j, h], out_ref.at[:, pl.ds(j * width + h * HD, HD)], sem.at[j, h]
                )
            )
            copies[-1].start()
    for copy in copies:
        copy.wait()


def finish_kernel(back_ref, normed_ref, mixed_ref, gq_ref, gk_ref, held, sem):
    width = normed_ref.shape[1]
    copies = [
        pltpu.make_async_copy(back_ref.at[:, pl.ds(width, width)], gq_ref, sem.at[0]),
        pltpu.make_async_copy(back_ref.at[:, pl.ds(2 * width, width)], gk_ref, sem.at[1]),
        pltpu.make_async_copy(held, mixed_ref, sem.at[2]),
    ]
    copies[0].start()
    copies[1].start()
    held[...] = (normed_ref[...].astype(F32) + back_ref[:, :width].astype(F32)).astype(BF16)
    copies[2].start()
    for copy in copies:
        copy.wait()


def per_device(
    query_space, key_space, value_space, query_time, key_time, cotangent, slot_clip, clip_res
):
    _, rows, channels = query_space.shape
    head_count = channels // HD
    frames = slot_clip.shape[0]
    full_channels = channels * lax.axis_size("head")
    positions_here = rows // lax.axis_size("frame")
    here = lax.axis_index("frame")

    def head_block(width=1):
        return pl.BlockSpec((rows, width * HD), lambda h: (0, h))

    def shared(shape):
        return pl.BlockSpec(shape, lambda h: (0,) * len(shape))

    def call(kernel, in_specs, out_specs, out_shape, flops=0, traffic=0):
        return pl.pallas_call(
            kernel,
            grid=(head_count,),
            in_specs=in_specs,
            out_specs=out_specs,
            out_shape=out_shape,
            compiler_params=pltpu.CompilerParams(
                dimension_semantics=("arbitrary",), vmem_limit_bytes=VMEM_BYTES
            ),
            cost_estimate=pl.CostEstimate(
                flops=flops, bytes_accessed=traffic, transcendentals=0
            ),
        )

    def local(kernel, in_specs, out_specs, out_shape, scratch, flops=0, traffic=0):
        return pl.pallas_call(
            kernel,
            in_specs=in_specs,
            out_specs=out_specs,
            out_shape=out_shape,
            scratch_shapes=scratch,
            compiler_params=pltpu.CompilerParams(vmem_limit_bytes=VMEM_BYTES),
            cost_estimate=pl.CostEstimate(
                flops=flops, bytes_accessed=traffic, transcendentals=0
            ),
        )

    def here_in(space, *arrays):
        return [pltpu.with_memory_space_constraint(array, space) for array in arrays]

    side = 8
    order = [z * side + y for y in Y_PLACES for z in Z_PLACES]
    numbers = jnp.arange(frames, dtype=jnp.int32)
    order_row = sum(
        jnp.where(numbers // side == i, y, 0) + jnp.where(numbers % side == i, side * z, 0)
        for i, (y, z) in enumerate(zip(Y_PLACES, Z_PLACES))
    )
    block_here = jnp.sum(jnp.where(order_row == here, numbers, 0))

    def ordered(per_frame):
        picked = order_row[:, None] == numbers[None, :]
        return jnp.sum(jnp.where(picked, per_frame[None, :], 0), axis=1)

    def exchange(array):
        width = array.shape[-1]
        blocks = array.reshape(frames, positions_here, width)
        moved = lax.all_to_all(
            blocks, "frame", split_axis=0, concat_axis=0, tiled=True, axis_index_groups=[order]
        )
        return moved.reshape(rows, width)

    whole = jax.ShapeDtypeStruct((rows, channels), BF16)
    product = 2 * rows * rows * HD * head_count
    size = rows * channels * 2

    q_space, k_space, v_space = query_space[0], key_space[0], value_space[0]

    hbm, vmem = pl.BlockSpec(memory_space=pltpu.HBM), pl.BlockSpec(memory_space=pltpu.VMEM)
    dma = pltpu.SemaphoreType.DMA
    packed = local(
        pack_kernel,
        [hbm] * 3,
        hbm,
        pltpu.HBM((rows, 3 * channels), BF16),
        [pltpu.VMEM((3, rows, channels), BF16), dma((3,)), dma((3,))],
        traffic=6 * size,
    )(*here_in(pltpu.HBM, query_time[0], key_time[0], cotangent[0]))
    moved = exchange(packed)

    clip_match = slot_clip[:, None] == jnp.arange(clip_res.shape[0], dtype=jnp.int32)[None, :]
    slot_res = jnp.sum(jnp.where(clip_match, clip_res[None, :], 0), axis=1)
    local_res = lax.dynamic_slice_in_dim(slot_res, here, 1, 0)
    live_space = jnp.arange(rows, dtype=jnp.int32) < local_res
    column = jnp.arange(HD, dtype=jnp.int32)[None, :]
    space_q_mask = jnp.broadcast_to(column == 0, (rows, HD)).astype(BF16)
    space_k_mask = jnp.where(live_space[:, None], 0.0, NEGATIVE).astype(BF16)
    space_k_mask = jnp.broadcast_to(space_k_mask, (rows, HD))
    place = jnp.arange(positions_here, dtype=jnp.int32)[None, :]
    live_time = (block_here * positions_here + place) < ordered(slot_res)[:, None]
    group = ordered(slot_clip)[:, None] * positions_here + place
    group = group.reshape(rows, 1)
    time_q_mask = (column == group).astype(BF16)
    time_k_mask = jnp.where((column == group) & live_time.reshape(rows, 1), 0.0, NEGATIVE)
    time_k_mask = time_k_mask.astype(BF16)
    live_row = live_time.reshape(1, rows).astype(F32)

    mask_spec = shared((rows, HD))
    space_out = call(
        space_forward_kernel,
        [head_block()] * 3 + [mask_spec, mask_spec, shared((rows, 1))],
        head_block(),
        jax.ShapeDtypeStruct((rows, channels), F32),
        flops=3 * product,
        traffic=5 * size,
    )(q_space, k_space, v_space, space_q_mask, space_k_mask, live_space[:, None].astype(F32))
    square_sum = lax.psum(jnp.sum(space_out * space_out, axis=-1), "head")
    inverse_rms = lax.rsqrt(square_sum / full_channels + EPSILON)
    normed_full = space_out * inverse_rms[:, None]
    normed = normed_full.astype(BF16)

    pair, shift = local(
        time_value_kernel,
        [vmem] * 5,
        [vmem, vmem],
        [pltpu.VMEM((rows, 2 * channels), BF16), pltpu.VMEM((8, rows), F32)],
        [],
        flops=3 * product,
        traffic=6 * size,
    )(*here_in(pltpu.VMEM, moved, normed, time_q_mask, time_k_mask, live_row))
    pair_moved = exchange(pair)
    results = local(
        time_rest_kernel,
        [vmem] * 5,
        hbm,
        pltpu.HBM((rows, 3 * channels), BF16),
        [pltpu.VMEM((3, head_count, rows, HD), BF16), dma((3, head_count))],
        flops=6 * product,
        traffic=8 * size,
    )(*here_in(pltpu.VMEM, moved, pair_moved, time_q_mask, time_k_mask, shift))
    back = exchange(results)

    grad_value_back = pair_moved[:, channels:]
    grad_in = jnp.where(live_space[:, None], cotangent[0], jnp.zeros_like(cotangent[0]))
    grad_norm = grad_in.astype(F32) + grad_value_back.astype(F32)
    inner_norm = lax.psum(jnp.sum(grad_norm * normed_full, axis=-1), "head")
    grad_space_out = (
        inverse_rms[:, None] * (grad_norm - normed_full * (inner_norm / full_channels)[:, None])
    ).astype(BF16)
    grad_query_space, grad_key_space, grad_value_space = call(
        space_backward_kernel,
        [head_block()] * 4 + [mask_spec, mask_spec],
        [head_block()] * 3,
        [whole] * 3,
        flops=6 * product,
        traffic=7 * size,
    )(q_space, k_space, v_space, grad_space_out, space_q_mask, space_k_mask)

    mixed, grad_query_time, grad_key_time = local(
        finish_kernel,
        [vmem] * 2,
        [hbm] * 3,
        [pltpu.HBM((rows, channels), BF16)] * 3,
        [pltpu.VMEM((rows, channels), BF16), dma((3,))],
        traffic=7 * size,
    )(*here_in(pltpu.VMEM, back, normed))
    return (
        mixed[None],
        grad_query_space[None],
        grad_key_space[None],
        grad_value_space[None],
        grad_query_time[None],
        grad_key_time[None],
    )


def solution(mesh):
    sharded = P("frame", None, "head")
    return jax.shard_map(
        per_device,
        mesh=mesh,
        in_specs=(sharded,) * 6 + (P(), P()),
        out_specs=(sharded,) * 6,
        check_vma=False,
    )
```

```python
import jax
import jax.numpy as jnp
from jax import lax
from jax.experimental import pallas as pl
from jax.experimental.pallas import tpu as pltpu
from jax.sharding import PartitionSpec as P

HD = 128
NEGATIVE = -1e30
EPSILON = 1e-06
LOG2E = 1.4426950408889634
F32 = jnp.float32
BF16 = jnp.bfloat16
VMEM_BYTES = 24 * 1024 * 1024
LOWEST = -3e38
Z_PLACES = (4, 5, 6, 7, 0, 1, 2, 3)
Y_PLACES = (4, 5, 6, 7, 0, 1, 2, 3)


def dot(a, b, ca, cb):
    return lax.dot_general(a, b, (((ca,), (cb,)), ((), ())), preferred_element_type=F32)


def softmax_keys_first(q, k, q_mask, k_mask):
    scale = HD ** (-0.5)
    scores = dot(
        jnp.concatenate([k, k_mask], axis=1), jnp.concatenate([q, q_mask], axis=1), 1, 1
    )
    highest = jnp.max(scores, axis=0, keepdims=True)
    expanded = jnp.exp2((scores - highest) * (scale * LOG2E))
    return expanded, 1.0 / jnp.sum(expanded, axis=0, keepdims=True)


def softmax_queries_first(q, k, q_mask, k_mask):
    scale = HD ** (-0.5)
    scores = dot(
        jnp.concatenate([q, q_mask], axis=1), jnp.concatenate([k, k_mask], axis=1), 1, 1
    )
    highest = jnp.max(scores, axis=1, keepdims=True)
    expanded = jnp.exp2((scores - highest) * (scale * LOG2E))
    return expanded, 1.0 / jnp.sum(expanded, axis=1, keepdims=True)


def pack_kernel(a_ref, b_ref, c_ref, out_ref, held, in_sem, out_sem):
    width = a_ref.shape[1]
    loads, stores = [], []
    for i, ref in enumerate((a_ref, b_ref, c_ref)):
        loads.append(pltpu.make_async_copy(ref, held.at[i], in_sem.at[i]))
        stores.append(
            pltpu.make_async_copy(
                held.at[i], out_ref.at[:, pl.ds(i * width, width)], out_sem.at[i]
            )
        )
    for load in loads:
        load.start()
    for load, store in zip(loads, stores):
        load.wait()
        store.start()
    for store in stores:
        store.wait()


def space_forward_kernel(q_ref, k_ref, v_ref, q_mask_ref, k_mask_ref, live_ref, out_ref):
    expanded, inverse = softmax_queries_first(
        q_ref[...], k_ref[...], q_mask_ref[...], k_mask_ref[...]
    )
    weights = (expanded * inverse).astype(BF16)
    out_ref[...] = dot(weights, v_ref[...], 1, 0) * live_ref[...]


def space_backward_kernel(
    q_ref, k_ref, v_ref, g_ref, q_mask_ref, k_mask_ref, gq_ref, gk_ref, gv_ref
):
    scale = HD ** (-0.5)
    q, k, v, g = q_ref[...], k_ref[...], v_ref[...], g_ref[...]
    expanded, inverse = softmax_keys_first(q, k, q_mask_ref[...], k_mask_ref[...])
    weights = expanded * inverse
    gv_ref[...] = dot(weights.astype(BF16), g, 1, 0).astype(BF16)
    grad_weights = dot(v, g, 1, 1)
    inner = jnp.sum(weights * grad_weights, axis=0, keepdims=True)
    grad_scores = (weights * (grad_weights - inner) * scale).astype(BF16)
    gk_ref[...] = dot(grad_scores, q, 1, 0).astype(BF16)
    gq_ref[...] = dot(grad_scores, k, 0, 0).astype(BF16)


def time_value_kernel(
    moved_ref, normed_ref, q_mask_ref, k_mask_ref, live_ref, out_ref, shift_ref
):
    scale = HD ** (-0.5) * LOG2E
    width = normed_ref.shape[1]
    out_ref[:, :width] = normed_ref[...]
    q_mask, k_mask, live = q_mask_ref[...], k_mask_ref[...], live_ref[...]
    for h in range(width // HD):
        q, k, g = (
            moved_ref[:, j * width + h * HD : j * width + (h + 1) * HD] for j in range(3)
        )
        scores = dot(
            jnp.concatenate([k, k_mask], axis=1), jnp.concatenate([q, q_mask], axis=1), 1, 1
        )
        highest = jnp.max(scores, axis=0, keepdims=True)
        expanded = jnp.exp2((scores - highest) * scale)
        inverse = 1.0 / jnp.sum(expanded, axis=0, keepdims=True)
        weights = (expanded * (inverse * live)).astype(BF16)
        shift_ref[h : h + 1, :] = jnp.where(
            live > 0, jnp.log2(inverse) - highest * scale, LOWEST
        )
        out_ref[:, width + h * HD : width + (h + 1) * HD] = dot(weights, g, 1, 0).astype(BF16)


def time_rest_kernel(
    moved_ref, pair_ref, q_mask_ref, k_mask_ref, shift_ref, out_ref, held, sem
):
    scale = HD ** (-0.5)
    width = pair_ref.shape[1] // 2
    heads = range(width // HD)
    copies = []
    q_mask, k_mask = q_mask_ref[...], k_mask_ref[...]

    def moved(j, h):
        return moved_ref[:, j * width + h * HD : j * width + (h + 1) * HD]

    def values(h):
        return pair_ref[:, h * HD : (h + 1) * HD]

    def send(j, h, result):
        held[j, h] = result.astype(BF16)
        copies.append(
            pltpu.make_async_copy(
                held.at[j, h], out_ref.at[:, pl.ds(j * width + h * HD, HD)], sem.at[j, h]
            )
        )
        copies[-1].start()

    weights = []
    for h in heads:
        scores = dot(
            jnp.concatenate([moved(1, h), k_mask], axis=1),
            jnp.concatenate([moved(0, h), q_mask], axis=1),
            1,
            1,
        )
        weights.append(jnp.exp2(scores * (scale * LOG2E) + shift_ref[h : h + 1, :]))
    grad_weights = [dot(values(h), moved(2, h), 1, 1) for h in heads]
    for h in heads:
        send(0, h, dot(weights[h].astype(BF16), values(h), 0, 0))
    grad_scores = []
    for h in heads:
        inner = jnp.sum(weights[h] * grad_weights[h], axis=0, keepdims=True)
        grad_scores.append((weights[h] * (grad_weights[h] - inner)).astype(BF16))
    for h in heads:
        send(1, h, dot(grad_scores[h], moved(1, h), 0, 0) * scale)
        send(2, h, dot(grad_scores[h], moved(0, h), 1, 0) * scale)
    for copy in copies:
        copy.wait()


def finish_kernel(back_ref, normed_ref, mixed_ref, gq_ref, gk_ref, held, sem):
    width = normed_ref.shape[1]
    copies = [
        pltpu.make_async_copy(back_ref.at[:, pl.ds(width, width)], gq_ref, sem.at[0]),
        pltpu.make_async_copy(back_ref.at[:, pl.ds(2 * width, width)], gk_ref, sem.at[1]),
        pltpu.make_async_copy(held, mixed_ref, sem.at[2]),
    ]
    copies[0].start()
    copies[1].start()
    held[...] = (normed_ref[...].astype(F32) + back_ref[:, :width].astype(F32)).astype(BF16)
    copies[2].start()
    for copy in copies:
        copy.wait()


def per_device(
    query_space, key_space, value_space, query_time, key_time, cotangent, slot_clip, clip_res
):
    _, rows, channels = query_space.shape
    head_count = channels // HD
    frames = slot_clip.shape[0]
    full_channels = channels * lax.axis_size("head")
    positions_here = rows // lax.axis_size("frame")
    here = lax.axis_index("frame")

    def head_block(width=1):
        return pl.BlockSpec((rows, width * HD), lambda h: (0, h))

    def shared(shape):
        return pl.BlockSpec(shape, lambda h: (0,) * len(shape))

    def call(kernel, in_specs, out_specs, out_shape, flops=0, traffic=0):
        return pl.pallas_call(
            kernel,
            grid=(head_count,),
            in_specs=in_specs,
            out_specs=out_specs,
            out_shape=out_shape,
            compiler_params=pltpu.CompilerParams(
                dimension_semantics=("arbitrary",), vmem_limit_bytes=VMEM_BYTES
            ),
            cost_estimate=pl.CostEstimate(
                flops=flops, bytes_accessed=traffic, transcendentals=0
            ),
        )

    def local(kernel, in_specs, out_specs, out_shape, scratch, flops=0, traffic=0):
        return pl.pallas_call(
            kernel,
            in_specs=in_specs,
            out_specs=out_specs,
            out_shape=out_shape,
            scratch_shapes=scratch,
            compiler_params=pltpu.CompilerParams(vmem_limit_bytes=VMEM_BYTES),
            cost_estimate=pl.CostEstimate(
                flops=flops, bytes_accessed=traffic, transcendentals=0
            ),
        )

    def here_in(space, *arrays):
        return [pltpu.with_memory_space_constraint(array, space) for array in arrays]

    side = 8
    order = [z * side + y for z in Z_PLACES for y in Y_PLACES]
    numbers = jnp.arange(frames, dtype=jnp.int32)
    order_row = sum(
        jnp.where(numbers // side == i, side * z, 0) + jnp.where(numbers % side == i, y, 0)
        for i, (y, z) in enumerate(zip(Y_PLACES, Z_PLACES))
    )
    block_here = jnp.sum(jnp.where(order_row == here, numbers, 0))

    def ordered(per_frame):
        picked = order_row[:, None] == numbers[None, :]
        return jnp.sum(jnp.where(picked, per_frame[None, :], 0), axis=1)

    def exchange(array):
        width = array.shape[-1]
        blocks = array.reshape(frames, positions_here, width)
        moved = lax.all_to_all(
            blocks, "frame", split_axis=0, concat_axis=0, tiled=True, axis_index_groups=[order]
        )
        return moved.reshape(rows, width)

    whole = jax.ShapeDtypeStruct((rows, channels), BF16)
    product = 2 * rows * rows * HD * head_count
    size = rows * channels * 2

    q_space, k_space, v_space = query_space[0], key_space[0], value_space[0]

    hbm, vmem = pl.BlockSpec(memory_space=pltpu.HBM), pl.BlockSpec(memory_space=pltpu.VMEM)
    dma = pltpu.SemaphoreType.DMA
    packed = local(
        pack_kernel,
        [hbm] * 3,
        hbm,
        pltpu.HBM((rows, 3 * channels), BF16),
        [pltpu.VMEM((3, rows, channels), BF16), dma((3,)), dma((3,))],
        traffic=6 * size,
    )(*here_in(pltpu.HBM, query_time[0], key_time[0], cotangent[0]))
    moved = exchange(packed)

    clip_match = slot_clip[:, None] == jnp.arange(clip_res.shape[0], dtype=jnp.int32)[None, :]
    slot_res = jnp.sum(jnp.where(clip_match, clip_res[None, :], 0), axis=1)
    local_res = lax.dynamic_slice_in_dim(slot_res, here, 1, 0)
    live_space = jnp.arange(rows, dtype=jnp.int32) < local_res
    column = jnp.arange(HD, dtype=jnp.int32)[None, :]
    space_q_mask = jnp.broadcast_to(column == 0, (rows, HD)).astype(BF16)
    space_k_mask = jnp.where(live_space[:, None], 0.0, NEGATIVE).astype(BF16)
    space_k_mask = jnp.broadcast_to(space_k_mask, (rows, HD))
    place = jnp.arange(positions_here, dtype=jnp.int32)[None, :]
    live_time = (block_here * positions_here + place) < ordered(slot_res)[:, None]
    group = ordered(slot_clip)[:, None] * positions_here + place
    group = group.reshape(rows, 1)
    time_q_mask = (column == group).astype(BF16)
    time_k_mask = jnp.where((column == group) & live_time.reshape(rows, 1), 0.0, NEGATIVE)
    time_k_mask = time_k_mask.astype(BF16)
    live_row = live_time.reshape(1, rows).astype(F32)

    mask_spec = shared((rows, HD))
    space_out = call(
        space_forward_kernel,
        [head_block()] * 3 + [mask_spec, mask_spec, shared((rows, 1))],
        head_block(),
        jax.ShapeDtypeStruct((rows, channels), F32),
        flops=3 * product,
        traffic=5 * size,
    )(q_space, k_space, v_space, space_q_mask, space_k_mask, live_space[:, None].astype(F32))
    square_sum = lax.psum(jnp.sum(space_out * space_out, axis=-1), "head")
    inverse_rms = lax.rsqrt(square_sum / full_channels + EPSILON)
    normed_full = space_out * inverse_rms[:, None]
    normed = normed_full.astype(BF16)

    pair, shift = local(
        time_value_kernel,
        [vmem] * 5,
        [vmem, vmem],
        [pltpu.VMEM((rows, 2 * channels), BF16), pltpu.VMEM((8, rows), F32)],
        [],
        flops=3 * product,
        traffic=6 * size,
    )(*here_in(pltpu.VMEM, moved, normed, time_q_mask, time_k_mask, live_row))
    pair_moved = exchange(pair)
    results = local(
        time_rest_kernel,
        [vmem] * 5,
        hbm,
        pltpu.HBM((rows, 3 * channels), BF16),
        [pltpu.VMEM((3, head_count, rows, HD), BF16), dma((3, head_count))],
        flops=6 * product,
        traffic=8 * size,
    )(*here_in(pltpu.VMEM, moved, pair_moved, time_q_mask, time_k_mask, shift))
    back = exchange(results)

    grad_value_back = pair_moved[:, channels:]
    grad_in = jnp.where(live_space[:, None], cotangent[0], jnp.zeros_like(cotangent[0]))
    grad_norm = grad_in.astype(F32) + grad_value_back.astype(F32)
    inner_norm = lax.psum(jnp.sum(grad_norm * normed_full, axis=-1), "head")
    grad_space_out = (
        inverse_rms[:, None] * (grad_norm - normed_full * (inner_norm / full_channels)[:, None])
    ).astype(BF16)
    grad_query_space, grad_key_space, grad_value_space = call(
        space_backward_kernel,
        [head_block()] * 4 + [mask_spec, mask_spec],
        [head_block()] * 3,
        [whole] * 3,
        flops=6 * product,
        traffic=7 * size,
    )(q_space, k_space, v_space, grad_space_out, space_q_mask, space_k_mask)

    mixed, grad_query_time, grad_key_time = local(
        finish_kernel,
        [vmem] * 2,
        [hbm] * 3,
        [pltpu.HBM((rows, channels), BF16)] * 3,
        [pltpu.VMEM((rows, channels), BF16), dma((3,))],
        traffic=7 * size,
    )(*here_in(pltpu.VMEM, back, normed))
    return (
        mixed[None],
        grad_query_space[None],
        grad_key_space[None],
        grad_value_space[None],
        grad_query_time[None],
        grad_key_time[None],
    )


def solution(mesh):
    sharded = P("frame", None, "head")
    return jax.shard_map(
        per_device,
        mesh=mesh,
        in_specs=(sharded,) * 6 + (P(), P()),
        out_specs=(sharded,) * 6,
        check_vma=False,
    )
```

```python
import jax
import jax.numpy as jnp
from jax import lax
from jax.experimental import pallas as pl
from jax.experimental.pallas import tpu as pltpu
from jax.sharding import PartitionSpec as P

HD = 128
NEGATIVE = -1e30
EPSILON = 1e-06
LOG2E = 1.4426950408889634
F32 = jnp.float32
BF16 = jnp.bfloat16
VMEM_BYTES = 24 * 1024 * 1024
LOWEST = -3e38
Z_PLACES = (4, 5, 6, 7, 0, 1, 2, 3)
Y_PLACES = (4, 5, 6, 7, 0, 1, 2, 3)


def dot(a, b, ca, cb):
    return lax.dot_general(a, b, (((ca,), (cb,)), ((), ())), preferred_element_type=F32)


def space_forward(
    q_ref, k_ref, v_ref, clip_ref, res_ref, out_ref, weights_ref, held, kept,
    clips, sizes, sem, core,
):
    @pl.when(lax.rem(lax.axis_index("head"), 2) == core)
    def _():
        copies = [
            pltpu.make_async_copy(ref, held.at[i], sem.at[i])
            for i, ref in enumerate((q_ref, k_ref, v_ref))
        ]
        small = [
            pltpu.make_async_copy(clip_ref, clips, sem.at[3]),
            pltpu.make_async_copy(res_ref, sizes, sem.at[4]),
        ]
        for copy in copies + small:
            copy.start()
        for copy in small:
            copy.wait()
        rows, width = out_ref.shape
        live_count = sizes[clips[lax.axis_index("frame")]]
        allowed = lax.broadcasted_iota(jnp.int32, (1, rows), 1) < live_count
        live = (lax.broadcasted_iota(jnp.int32, (rows, 1), 0) < live_count).astype(F32)
        scale = HD ** (-0.5) * LOG2E
        for copy in copies:
            copy.wait()
        for h in range(width // HD):
            q, k, v = (held[j, :, h * HD : (h + 1) * HD] for j in range(3))
            scores = jnp.where(allowed, dot(q, k, 1, 1), NEGATIVE)
            highest = jnp.max(scores, axis=1, keepdims=True)
            expanded = jnp.exp2((scores - highest) * scale)
            inverse = 1.0 / jnp.sum(expanded, axis=1, keepdims=True)
            weights = (expanded * inverse).astype(BF16)
            out_ref[:, h * HD : (h + 1) * HD] = dot(weights, v, 1, 0) * live
        allowed = lax.broadcasted_iota(jnp.int32, (rows, 1), 0) < live_count
        stores = []
        for h in range(width // HD):
            q, k = (held[j, :, h * HD : (h + 1) * HD] for j in range(2))
            scores = jnp.where(allowed, dot(k, q, 1, 1), NEGATIVE)
            highest = jnp.max(scores, axis=0, keepdims=True)
            expanded = jnp.exp2((scores - highest) * scale)
            inverse = 1.0 / jnp.sum(expanded, axis=0, keepdims=True)
            kept[h] = expanded * inverse
            stores.append(pltpu.make_async_copy(kept.at[h], weights_ref.at[h], sem.at[5 + h]))
            stores[-1].start()
        for store in stores:
            store.wait()


def pack_kernel(
    q_ref, k_ref, v_ref, clip_ref, res_ref, a_ref, b_ref, c_ref, packed_ref, out_ref,
    weights_ref, held, kept, clips, sizes, space_sem, in_sem, out_sem,
):
    space_forward(
        q_ref, k_ref, v_ref, clip_ref, res_ref, out_ref, weights_ref, held, kept, clips, sizes,
        space_sem, 0,
    )
    width = a_ref.shape[1]
    loads, stores = [], []
    for i, ref in enumerate((a_ref, b_ref, c_ref)):
        loads.append(pltpu.make_async_copy(ref, held.at[i], in_sem.at[i]))
        stores.append(
            pltpu.make_async_copy(
                held.at[i], packed_ref.at[:, pl.ds(i * width, width)], out_sem.at[i]
            )
        )
    for load in loads:
        load.start()
    for load, store in zip(loads, stores):
        load.wait()
        store.start()
    for store in stores:
        store.wait()


def space_rest_kernel(
    q_ref, k_ref, v_ref, clip_ref, res_ref, given_ref, given_weights_ref, out_ref, weights_ref,
    held, kept, clips, sizes, sem,
):
    space_forward(
        q_ref, k_ref, v_ref, clip_ref, res_ref, out_ref, weights_ref, held, kept, clips, sizes,
        sem, 1,
    )


def space_backward_kernel(q_ref, k_ref, v_ref, g_ref, weights_ref, gq_ref, gk_ref, gv_ref):
    scale = HD ** (-0.5)
    q, k, v, g = q_ref[...], k_ref[...], v_ref[...], g_ref[...]
    weights = weights_ref[0]
    gv_ref[...] = dot(weights.astype(BF16), g, 1, 0).astype(BF16)
    grad_weights = dot(v, g, 1, 1)
    inner = jnp.sum(weights * grad_weights, axis=0, keepdims=True)
    grad_scores = (weights * (grad_weights - inner) * scale).astype(BF16)
    gk_ref[...] = dot(grad_scores, q, 1, 0).astype(BF16)
    gq_ref[...] = dot(grad_scores, k, 0, 0).astype(BF16)


def time_value_kernel(
    moved_ref, normed_ref, q_mask_ref, k_mask_ref, live_ref, out_ref, shift_ref
):
    scale = HD ** (-0.5) * LOG2E
    width = normed_ref.shape[1]
    out_ref[:, :width] = normed_ref[...]
    q_mask, k_mask, live = q_mask_ref[...], k_mask_ref[...], live_ref[...]
    for h in range(width // HD):
        q, k, g = (
            moved_ref[:, j * width + h * HD : j * width + (h + 1) * HD] for j in range(3)
        )
        scores = dot(
            jnp.concatenate([k, k_mask], axis=1), jnp.concatenate([q, q_mask], axis=1), 1, 1
        )
        highest = jnp.max(scores, axis=0, keepdims=True)
        expanded = jnp.exp2((scores - highest) * scale)
        inverse = 1.0 / jnp.sum(expanded, axis=0, keepdims=True)
        weights = (expanded * (inverse * live)).astype(BF16)
        shift_ref[h : h + 1, :] = jnp.where(
            live > 0, jnp.log2(inverse) - highest * scale, LOWEST
        )
        out_ref[:, width + h * HD : width + (h + 1) * HD] = dot(weights, g, 1, 0).astype(BF16)


def time_rest_kernel(
    moved_ref, pair_ref, q_mask_ref, k_mask_ref, shift_ref, out_ref, held, sem
):
    scale = HD ** (-0.5)
    width = pair_ref.shape[1] // 2
    heads = range(width // HD)
    copies = []
    q_mask, k_mask = q_mask_ref[...], k_mask_ref[...]

    def moved(j, h):
        return moved_ref[:, j * width + h * HD : j * width + (h + 1) * HD]

    def values(h):
        return pair_ref[:, h * HD : (h + 1) * HD]

    def send(j, h, result):
        held[j, h] = result.astype(BF16)
        copies.append(
            pltpu.make_async_copy(
                held.at[j, h], out_ref.at[:, pl.ds(j * width + h * HD, HD)], sem.at[j, h]
            )
        )
        copies[-1].start()

    weights = []
    for h in heads:
        scores = dot(
            jnp.concatenate([moved(1, h), k_mask], axis=1),
            jnp.concatenate([moved(0, h), q_mask], axis=1),
            1,
            1,
        )
        weights.append(jnp.exp2(scores * (scale * LOG2E) + shift_ref[h : h + 1, :]))
    grad_weights = [dot(values(h), moved(2, h), 1, 1) for h in heads]
    for h in heads:
        send(0, h, dot(weights[h].astype(BF16), values(h), 0, 0))
    grad_scores = []
    for h in heads:
        inner = jnp.sum(weights[h] * grad_weights[h], axis=0, keepdims=True)
        grad_scores.append((weights[h] * (grad_weights[h] - inner)).astype(BF16))
    for h in heads:
        send(1, h, dot(grad_scores[h], moved(1, h), 0, 0) * scale)
        send(2, h, dot(grad_scores[h], moved(0, h), 1, 0) * scale)
    for copy in copies:
        copy.wait()


def finish_kernel(back_ref, normed_ref, mixed_ref, gq_ref, gk_ref, held, sem):
    width = normed_ref.shape[1]
    copies = [
        pltpu.make_async_copy(back_ref.at[:, pl.ds(width, width)], gq_ref, sem.at[0]),
        pltpu.make_async_copy(back_ref.at[:, pl.ds(2 * width, width)], gk_ref, sem.at[1]),
        pltpu.make_async_copy(held, mixed_ref, sem.at[2]),
    ]
    copies[0].start()
    copies[1].start()
    held[...] = (normed_ref[...].astype(F32) + back_ref[:, :width].astype(F32)).astype(BF16)
    copies[2].start()
    for copy in copies:
        copy.wait()


def per_device(
    query_space, key_space, value_space, query_time, key_time, cotangent, slot_clip, clip_res
):
    _, rows, channels = query_space.shape
    head_count = channels // HD
    frames = slot_clip.shape[0]
    full_channels = channels * lax.axis_size("head")
    positions_here = rows // lax.axis_size("frame")
    here = lax.axis_index("frame")

    def head_block(width=1):
        return pl.BlockSpec((rows, width * HD), lambda h: (0, h))

    def call(kernel, in_specs, out_specs, out_shape, flops=0, traffic=0):
        return pl.pallas_call(
            kernel,
            grid=(head_count,),
            in_specs=in_specs,
            out_specs=out_specs,
            out_shape=out_shape,
            compiler_params=pltpu.CompilerParams(
                dimension_semantics=("arbitrary",), vmem_limit_bytes=VMEM_BYTES
            ),
            cost_estimate=pl.CostEstimate(
                flops=flops, bytes_accessed=traffic, transcendentals=0
            ),
        )

    def local(
        kernel, in_specs, out_specs, out_shape, scratch, flops=0, traffic=0, aliases={}
    ):
        return pl.pallas_call(
            kernel,
            in_specs=in_specs,
            out_specs=out_specs,
            out_shape=out_shape,
            scratch_shapes=scratch,
            input_output_aliases=aliases,
            compiler_params=pltpu.CompilerParams(vmem_limit_bytes=VMEM_BYTES),
            cost_estimate=pl.CostEstimate(
                flops=flops, bytes_accessed=traffic, transcendentals=0
            ),
        )

    def here_in(space, *arrays):
        return [pltpu.with_memory_space_constraint(array, space) for array in arrays]

    side = 8
    order = [z * side + y for z in Z_PLACES for y in Y_PLACES]
    numbers = jnp.arange(frames, dtype=jnp.int32)
    order_row = sum(
        jnp.where(numbers // side == i, side * z, 0) + jnp.where(numbers % side == i, y, 0)
        for i, (y, z) in enumerate(zip(Y_PLACES, Z_PLACES))
    )
    block_here = jnp.sum(jnp.where(order_row == here, numbers, 0))

    def ordered(per_frame):
        picked = order_row[:, None] == numbers[None, :]
        return jnp.sum(jnp.where(picked, per_frame[None, :], 0), axis=1)

    def exchange(array):
        width = array.shape[-1]
        blocks = array.reshape(frames, positions_here, width)
        moved = lax.all_to_all(
            blocks, "frame", split_axis=0, concat_axis=0, tiled=True, axis_index_groups=[order]
        )
        return moved.reshape(rows, width)

    whole = jax.ShapeDtypeStruct((rows, channels), BF16)
    product = 2 * rows * rows * HD * head_count
    size = rows * channels * 2

    q_space, k_space, v_space = query_space[0], key_space[0], value_space[0]

    hbm, vmem = pl.BlockSpec(memory_space=pltpu.HBM), pl.BlockSpec(memory_space=pltpu.VMEM)
    dma = pltpu.SemaphoreType.DMA
    space = here_in(pltpu.HBM, q_space, k_space, v_space, slot_clip, clip_res)
    scalars = [pltpu.SMEM((frames,), jnp.int32), pltpu.SMEM(clip_res.shape, jnp.int32)]
    kept = [
        pltpu.VMEM((rows, channels), F32),
        pltpu.HBM((head_count, rows, rows), F32),
    ]
    weights_held = pltpu.VMEM((head_count, rows, rows), F32)
    space_sems = dma((5 + head_count,))
    packed, space_out, space_weights = local(
        pack_kernel,
        [hbm] * 8,
        [hbm, vmem, hbm],
        [pltpu.HBM((rows, 3 * channels), BF16)] + kept,
        [pltpu.VMEM((3, rows, channels), BF16), weights_held, *scalars, space_sems, dma((3,)), dma((3,))],
        traffic=6 * size,
    )(*space, *here_in(pltpu.HBM, query_time[0], key_time[0], cotangent[0]))
    moved = exchange(packed)

    clip_match = slot_clip[:, None] == jnp.arange(clip_res.shape[0], dtype=jnp.int32)[None, :]
    slot_res = jnp.sum(jnp.where(clip_match, clip_res[None, :], 0), axis=1)
    local_res = lax.dynamic_slice_in_dim(slot_res, here, 1, 0)
    live_space = jnp.arange(rows, dtype=jnp.int32) < local_res
    column = jnp.arange(HD, dtype=jnp.int32)[None, :]
    place = jnp.arange(positions_here, dtype=jnp.int32)[None, :]
    live_time = (block_here * positions_here + place) < ordered(slot_res)[:, None]
    group = ordered(slot_clip)[:, None] * positions_here + place
    group = group.reshape(rows, 1)
    time_q_mask = (column == group).astype(BF16)
    time_k_mask = jnp.where((column == group) & live_time.reshape(rows, 1), 0.0, NEGATIVE)
    time_k_mask = time_k_mask.astype(BF16)
    live_row = live_time.reshape(1, rows).astype(F32)

    space_out, space_weights = local(
        space_rest_kernel,
        [hbm] * 5 + [vmem, hbm],
        [vmem, hbm],
        kept,
        [pltpu.VMEM((3, rows, channels), BF16), weights_held, *scalars, space_sems],
        flops=2 * product,
        traffic=5 * size,
        aliases={5: 0, 6: 1},
    )(*space, *here_in(pltpu.VMEM, space_out), *here_in(pltpu.HBM, space_weights))
    square_sum = lax.psum(jnp.sum(space_out * space_out, axis=-1), "head")
    inverse_rms = lax.rsqrt(square_sum / full_channels + EPSILON)
    normed_full = space_out * inverse_rms[:, None]
    normed = normed_full.astype(BF16)

    pair, shift = local(
        time_value_kernel,
        [vmem] * 5,
        [vmem, vmem],
        [pltpu.VMEM((rows, 2 * channels), BF16), pltpu.VMEM((8, rows), F32)],
        [],
        flops=3 * product,
        traffic=6 * size,
    )(*here_in(pltpu.VMEM, moved, normed, time_q_mask, time_k_mask, live_row))
    pair_moved = exchange(pair)
    results = local(
        time_rest_kernel,
        [vmem] * 5,
        hbm,
        pltpu.HBM((rows, 3 * channels), BF16),
        [pltpu.VMEM((3, head_count, rows, HD), BF16), dma((3, head_count))],
        flops=6 * product,
        traffic=8 * size,
    )(*here_in(pltpu.VMEM, moved, pair_moved, time_q_mask, time_k_mask, shift))
    back = exchange(results)

    grad_value_back = pair_moved[:, channels:]
    grad_in = jnp.where(live_space[:, None], cotangent[0], jnp.zeros_like(cotangent[0]))
    grad_norm = grad_in.astype(F32) + grad_value_back.astype(F32)
    inner_norm = lax.psum(jnp.sum(grad_norm * normed_full, axis=-1), "head")
    grad_space_out = (
        inverse_rms[:, None] * (grad_norm - normed_full * (inner_norm / full_channels)[:, None])
    ).astype(BF16)
    grad_query_space, grad_key_space, grad_value_space = call(
        space_backward_kernel,
        [head_block()] * 4 + [pl.BlockSpec((1, rows, rows), lambda h: (h, 0, 0))],
        [head_block()] * 3,
        [whole] * 3,
        flops=4 * product,
        traffic=15 * size,
    )(q_space, k_space, v_space, grad_space_out, *here_in(pltpu.HBM, space_weights))

    mixed, grad_query_time, grad_key_time = local(
        finish_kernel,
        [vmem] * 2,
        [hbm] * 3,
        [pltpu.HBM((rows, channels), BF16)] * 3,
        [pltpu.VMEM((rows, channels), BF16), dma((3,))],
        traffic=7 * size,
    )(*here_in(pltpu.VMEM, back, normed))
    return (
        mixed[None],
        grad_query_space[None],
        grad_key_space[None],
        grad_value_space[None],
        grad_query_time[None],
        grad_key_time[None],
    )


def solution(mesh):
    sharded = P("frame", None, "head")
    return jax.shard_map(
        per_device,
        mesh=mesh,
        in_specs=(sharded,) * 6 + (P(), P()),
        out_specs=(sharded,) * 6,
        check_vma=False,
    )
```

```python
import jax
import jax.numpy as jnp
from jax import lax
from jax.experimental import pallas as pl
from jax.experimental.pallas import tpu as pltpu
from jax.sharding import PartitionSpec as P

HD = 128
NEGATIVE = -1e30
EPSILON = 1e-06
LOG2E = 1.4426950408889634
F32 = jnp.float32
BF16 = jnp.bfloat16
VMEM_BYTES = 24 * 1024 * 1024
LOWEST = -3e38
Z_PLACES = (5, 6, 7, 0, 1, 2, 3, 4)
Y_PLACES = (4, 5, 6, 7, 0, 1, 2, 3)


def dot(a, b, ca, cb):
    return lax.dot_general(a, b, (((ca,), (cb,)), ((), ())), preferred_element_type=F32)


def space_forward(
    q_ref, k_ref, v_ref, clip_ref, res_ref, out_ref, weights_ref, held, kept,
    clips, sizes, sem, core,
):
    @pl.when(lax.rem(lax.axis_index("head"), 2) == core)
    def _():
        copies = [
            pltpu.make_async_copy(ref, held.at[i], sem.at[i])
            for i, ref in enumerate((q_ref, k_ref, v_ref))
        ]
        small = [
            pltpu.make_async_copy(clip_ref, clips, sem.at[3]),
            pltpu.make_async_copy(res_ref, sizes, sem.at[4]),
        ]
        for copy in copies + small:
            copy.start()
        for copy in small:
            copy.wait()
        rows, width = out_ref.shape
        live_count = sizes[clips[lax.axis_index("frame")]]
        allowed = lax.broadcasted_iota(jnp.int32, (1, rows), 1) < live_count
        live = (lax.broadcasted_iota(jnp.int32, (rows, 1), 0) < live_count).astype(F32)
        scale = HD ** (-0.5) * LOG2E
        for copy in copies:
            copy.wait()
        for h in range(width // HD):
            q, k, v = (held[j, :, h * HD : (h + 1) * HD] for j in range(3))
            scores = jnp.where(allowed, dot(q, k, 1, 1), NEGATIVE)
            highest = jnp.max(scores, axis=1, keepdims=True)
            expanded = jnp.exp2((scores - highest) * scale)
            inverse = 1.0 / jnp.sum(expanded, axis=1, keepdims=True)
            weights = (expanded * inverse).astype(BF16)
            out_ref[:, h * HD : (h + 1) * HD] = dot(weights, v, 1, 0) * live
        allowed = lax.broadcasted_iota(jnp.int32, (rows, 1), 0) < live_count
        stores = []
        for h in range(width // HD):
            q, k = (held[j, :, h * HD : (h + 1) * HD] for j in range(2))
            scores = jnp.where(allowed, dot(k, q, 1, 1), NEGATIVE)
            highest = jnp.max(scores, axis=0, keepdims=True)
            expanded = jnp.exp2((scores - highest) * scale)
            inverse = 1.0 / jnp.sum(expanded, axis=0, keepdims=True)
            kept[h] = expanded * inverse
            stores.append(pltpu.make_async_copy(kept.at[h], weights_ref.at[h], sem.at[5 + h]))
            stores[-1].start()
        for store in stores:
            store.wait()


def pack_kernel(
    q_ref, k_ref, v_ref, clip_ref, res_ref, a_ref, b_ref, c_ref, packed_ref, out_ref,
    weights_ref, held, kept, clips, sizes, space_sem, in_sem, out_sem,
):
    space_forward(
        q_ref, k_ref, v_ref, clip_ref, res_ref, out_ref, weights_ref, held, kept, clips, sizes,
        space_sem, 0,
    )
    width = a_ref.shape[1]
    loads, stores = [], []
    for i, ref in enumerate((a_ref, b_ref, c_ref)):
        loads.append(pltpu.make_async_copy(ref, held.at[i], in_sem.at[i]))
        stores.append(
            pltpu.make_async_copy(
                held.at[i], packed_ref.at[:, pl.ds(i * width, width)], out_sem.at[i]
            )
        )
    for load in loads:
        load.start()
    for load, store in zip(loads, stores):
        load.wait()
        store.start()
    for store in stores:
        store.wait()


def space_rest_kernel(
    q_ref, k_ref, v_ref, clip_ref, res_ref, given_ref, given_weights_ref, out_ref, weights_ref,
    held, kept, clips, sizes, sem,
):
    space_forward(
        q_ref, k_ref, v_ref, clip_ref, res_ref, out_ref, weights_ref, held, kept, clips, sizes,
        sem, 1,
    )


def space_backward_kernel(q_ref, k_ref, v_ref, g_ref, weights_ref, gq_ref, gk_ref, gv_ref):
    scale = HD ** (-0.5)
    q, k, v, g = q_ref[...], k_ref[...], v_ref[...], g_ref[...]
    weights = weights_ref[0]
    gv_ref[...] = dot(weights.astype(BF16), g, 1, 0).astype(BF16)
    grad_weights = dot(v, g, 1, 1)
    inner = jnp.sum(weights * grad_weights, axis=0, keepdims=True)
    grad_scores = (weights * (grad_weights - inner) * scale).astype(BF16)
    gk_ref[...] = dot(grad_scores, q, 1, 0).astype(BF16)
    gq_ref[...] = dot(grad_scores, k, 0, 0).astype(BF16)


def time_value_kernel(
    moved_ref, normed_ref, q_mask_ref, k_mask_ref, live_ref, out_ref, shift_ref
):
    scale = HD ** (-0.5) * LOG2E
    width = normed_ref.shape[1]
    out_ref[:, :width] = normed_ref[...]
    q_mask, k_mask, live = q_mask_ref[...], k_mask_ref[...], live_ref[...]
    heads = range(width // HD)

    def moved(j, h):
        return moved_ref[:, j * width + h * HD : j * width + (h + 1) * HD]

    scores = [
        dot(
            jnp.concatenate([moved(1, h), k_mask], axis=1),
            jnp.concatenate([moved(0, h), q_mask], axis=1),
            1,
            1,
        )
        for h in heads
    ]
    for h in heads:
        highest = jnp.max(scores[h], axis=0, keepdims=True)
        expanded = jnp.exp2((scores[h] - highest) * scale)
        inverse = 1.0 / jnp.sum(expanded, axis=0, keepdims=True)
        weights = (expanded * (inverse * live)).astype(BF16)
        shift_ref[h : h + 1, :] = jnp.where(
            live > 0, jnp.log2(inverse) - highest * scale, LOWEST
        )
        grad_value = dot(weights, moved(2, h), 1, 0)
        out_ref[:, width + h * HD : width + (h + 1) * HD] = grad_value.astype(BF16)


def time_rest_kernel(
    moved_ref, pair_ref, q_mask_ref, k_mask_ref, shift_ref, out_ref, held, sem
):
    scale = HD ** (-0.5)
    width = pair_ref.shape[1] // 2
    heads = range(width // HD)
    copies = []
    q_mask, k_mask = q_mask_ref[...], k_mask_ref[...]

    def moved(j, h):
        return moved_ref[:, j * width + h * HD : j * width + (h + 1) * HD]

    def values(h):
        return pair_ref[:, h * HD : (h + 1) * HD]

    def send(j, h, result):
        held[j, h] = result.astype(BF16)
        copies.append(
            pltpu.make_async_copy(
                held.at[j, h], out_ref.at[:, pl.ds(j * width + h * HD, HD)], sem.at[j, h]
            )
        )
        copies[-1].start()

    weights = []
    for h in heads:
        scores = dot(
            jnp.concatenate([moved(1, h), k_mask], axis=1),
            jnp.concatenate([moved(0, h), q_mask], axis=1),
            1,
            1,
        )
        weights.append(jnp.exp2(scores * (scale * LOG2E) + shift_ref[h : h + 1, :]))
    grad_weights = [dot(values(h), moved(2, h), 1, 1) for h in heads]
    for h in heads:
        send(0, h, dot(weights[h].astype(BF16), values(h), 0, 0))
    grad_scores = []
    for h in heads:
        inner = jnp.sum(weights[h] * grad_weights[h], axis=0, keepdims=True)
        grad_scores.append((weights[h] * (grad_weights[h] - inner)).astype(BF16))
    for h in heads:
        send(1, h, dot(grad_scores[h], moved(1, h), 0, 0) * scale)
        send(2, h, dot(grad_scores[h], moved(0, h), 1, 0) * scale)
    for copy in copies:
        copy.wait()


def finish_kernel(back_ref, normed_ref, mixed_ref, gq_ref, gk_ref, held, sem):
    width = normed_ref.shape[1]
    copies = [
        pltpu.make_async_copy(back_ref.at[:, pl.ds(width, width)], gq_ref, sem.at[0]),
        pltpu.make_async_copy(back_ref.at[:, pl.ds(2 * width, width)], gk_ref, sem.at[1]),
        pltpu.make_async_copy(held, mixed_ref, sem.at[2]),
    ]
    copies[0].start()
    copies[1].start()
    held[...] = (normed_ref[...].astype(F32) + back_ref[:, :width].astype(F32)).astype(BF16)
    copies[2].start()
    for copy in copies:
        copy.wait()


def per_device(
    query_space, key_space, value_space, query_time, key_time, cotangent, slot_clip, clip_res
):
    _, rows, channels = query_space.shape
    head_count = channels // HD
    frames = slot_clip.shape[0]
    full_channels = channels * lax.axis_size("head")
    positions_here = rows // lax.axis_size("frame")
    here = lax.axis_index("frame")

    def head_block(width=1):
        return pl.BlockSpec((rows, width * HD), lambda h: (0, h))

    def call(kernel, in_specs, out_specs, out_shape, flops=0, traffic=0):
        return pl.pallas_call(
            kernel,
            grid=(head_count,),
            in_specs=in_specs,
            out_specs=out_specs,
            out_shape=out_shape,
            compiler_params=pltpu.CompilerParams(
                dimension_semantics=("arbitrary",), vmem_limit_bytes=VMEM_BYTES
            ),
            cost_estimate=pl.CostEstimate(
                flops=flops, bytes_accessed=traffic, transcendentals=0
            ),
        )

    def local(
        kernel, in_specs, out_specs, out_shape, scratch, flops=0, traffic=0, aliases={}
    ):
        return pl.pallas_call(
            kernel,
            in_specs=in_specs,
            out_specs=out_specs,
            out_shape=out_shape,
            scratch_shapes=scratch,
            input_output_aliases=aliases,
            compiler_params=pltpu.CompilerParams(vmem_limit_bytes=VMEM_BYTES),
            cost_estimate=pl.CostEstimate(
                flops=flops, bytes_accessed=traffic, transcendentals=0
            ),
        )

    def here_in(space, *arrays):
        return [pltpu.with_memory_space_constraint(array, space) for array in arrays]

    side = 8
    order = [z * side + y for z in Z_PLACES for y in Y_PLACES]
    numbers = jnp.arange(frames, dtype=jnp.int32)
    order_row = sum(
        jnp.where(numbers // side == i, side * z, 0) + jnp.where(numbers % side == i, y, 0)
        for i, (y, z) in enumerate(zip(Y_PLACES, Z_PLACES))
    )
    block_here = jnp.sum(jnp.where(order_row == here, numbers, 0))

    def ordered(per_frame):
        picked = order_row[:, None] == numbers[None, :]
        return jnp.sum(jnp.where(picked, per_frame[None, :], 0), axis=1)

    def exchange(array):
        width = array.shape[-1]
        blocks = array.reshape(frames, positions_here, width)
        moved = lax.all_to_all(
            blocks, "frame", split_axis=0, concat_axis=0, tiled=True, axis_index_groups=[order]
        )
        return moved.reshape(rows, width)

    whole = jax.ShapeDtypeStruct((rows, channels), BF16)
    product = 2 * rows * rows * HD * head_count
    size = rows * channels * 2

    q_space, k_space, v_space = query_space[0], key_space[0], value_space[0]

    hbm, vmem = pl.BlockSpec(memory_space=pltpu.HBM), pl.BlockSpec(memory_space=pltpu.VMEM)
    dma = pltpu.SemaphoreType.DMA
    space = here_in(pltpu.HBM, q_space, k_space, v_space, slot_clip, clip_res)
    scalars = [pltpu.SMEM((frames,), jnp.int32), pltpu.SMEM(clip_res.shape, jnp.int32)]
    kept = [
        pltpu.VMEM((rows, channels), F32),
        pltpu.HBM((head_count, rows, rows), F32),
    ]
    weights_held = pltpu.VMEM((head_count, rows, rows), F32)
    space_sems = dma((5 + head_count,))
    packed, space_out, space_weights = local(
        pack_kernel,
        [hbm] * 8,
        [hbm, vmem, hbm],
        [pltpu.HBM((rows, 3 * channels), BF16)] + kept,
        [pltpu.VMEM((3, rows, channels), BF16), weights_held, *scalars, space_sems, dma((3,)), dma((3,))],
        traffic=6 * size,
    )(*space, *here_in(pltpu.HBM, query_time[0], key_time[0], cotangent[0]))
    moved = exchange(packed)

    clip_match = slot_clip[:, None] == jnp.arange(clip_res.shape[0], dtype=jnp.int32)[None, :]
    slot_res = jnp.sum(jnp.where(clip_match, clip_res[None, :], 0), axis=1)
    local_res = lax.dynamic_slice_in_dim(slot_res, here, 1, 0)
    live_space = jnp.arange(rows, dtype=jnp.int32) < local_res
    column = jnp.arange(HD, dtype=jnp.int32)[None, :]
    place = jnp.arange(positions_here, dtype=jnp.int32)[None, :]
    live_time = (block_here * positions_here + place) < ordered(slot_res)[:, None]
    group = ordered(slot_clip)[:, None] * positions_here + place
    group = group.reshape(rows, 1)
    time_q_mask = (column == group).astype(BF16)
    time_k_mask = jnp.where((column == group) & live_time.reshape(rows, 1), 0.0, NEGATIVE)
    time_k_mask = time_k_mask.astype(BF16)
    live_row = live_time.reshape(1, rows).astype(F32)

    space_out, space_weights = local(
        space_rest_kernel,
        [hbm] * 5 + [vmem, hbm],
        [vmem, hbm],
        kept,
        [pltpu.VMEM((3, rows, channels), BF16), weights_held, *scalars, space_sems],
        flops=2 * product,
        traffic=5 * size,
        aliases={5: 0, 6: 1},
    )(*space, *here_in(pltpu.VMEM, space_out), *here_in(pltpu.HBM, space_weights))
    square_sum = lax.psum(jnp.sum(space_out * space_out, axis=-1), "head")
    inverse_rms = lax.rsqrt(square_sum / full_channels + EPSILON)
    normed_full = space_out * inverse_rms[:, None]
    normed = normed_full.astype(BF16)

    pair, shift = local(
        time_value_kernel,
        [vmem] * 5,
        [vmem, vmem],
        [pltpu.VMEM((rows, 2 * channels), BF16), pltpu.VMEM((8, rows), F32)],
        [],
        flops=3 * product,
        traffic=6 * size,
    )(*here_in(pltpu.VMEM, moved, normed, time_q_mask, time_k_mask, live_row))
    pair_moved = exchange(pair)
    results = local(
        time_rest_kernel,
        [vmem] * 5,
        hbm,
        pltpu.HBM((rows, 3 * channels), BF16),
        [pltpu.VMEM((3, head_count, rows, HD), BF16), dma((3, head_count))],
        flops=6 * product,
        traffic=8 * size,
    )(*here_in(pltpu.VMEM, moved, pair_moved, time_q_mask, time_k_mask, shift))
    back = exchange(results)

    grad_value_back = pair_moved[:, channels:]
    grad_in = jnp.where(live_space[:, None], cotangent[0], jnp.zeros_like(cotangent[0]))
    grad_norm = grad_in.astype(F32) + grad_value_back.astype(F32)
    inner_norm = lax.psum(jnp.sum(grad_norm * normed_full, axis=-1), "head")
    grad_space_out = (
        inverse_rms[:, None] * (grad_norm - normed_full * (inner_norm / full_channels)[:, None])
    ).astype(BF16)
    grad_query_space, grad_key_space, grad_value_space = call(
        space_backward_kernel,
        [head_block()] * 4 + [pl.BlockSpec((1, rows, rows), lambda h: (h, 0, 0))],
        [head_block()] * 3,
        [whole] * 3,
        flops=4 * product,
        traffic=15 * size,
    )(q_space, k_space, v_space, grad_space_out, *here_in(pltpu.HBM, space_weights))

    mixed, grad_query_time, grad_key_time = local(
        finish_kernel,
        [vmem] * 2,
        [hbm] * 3,
        [pltpu.HBM((rows, channels), BF16)] * 3,
        [pltpu.VMEM((rows, channels), BF16), dma((3,))],
        traffic=7 * size,
    )(*here_in(pltpu.VMEM, back, normed))
    return (
        mixed[None],
        grad_query_space[None],
        grad_key_space[None],
        grad_value_space[None],
        grad_query_time[None],
        grad_key_time[None],
    )


def solution(mesh):
    sharded = P("frame", None, "head")
    return jax.shard_map(
        per_device,
        mesh=mesh,
        in_specs=(sharded,) * 6 + (P(), P()),
        out_specs=(sharded,) * 6,
        check_vma=False,
    )
```
